32 devices in a mesh: row: 4 (over z), col: 8 (over y, x, core).
Axes of the slice: x: 2, y: 2, z: 4, core: 2. Of those that a mesh axis runs over, the one named last changes fastest.
Arguments:
- eigvecs: bfloat16 [2048, 16384], P('row', 'col'), may hold values from -0.01171875 to 0.01171875
- pole_order: int32 [16384], P('col'), may hold values from 0 to 16383, as said below
- pole_weight: float32 [16384], P('col'), may hold values from 0.17 to 6
- root_gap: int32 [2048], replicated, may hold values from 1024 to 15358, as said below
- root_shift: float32 [2048], replicated, may hold values from -0.25 to 0.25
- column_weight: float32 [2048], replicated, may hold values from 4 to 40
- panel_vectors: bfloat16 [2, 2048, 256], P(None, 'row'), may hold values from -0.125 to 0.125
- panel_factors: float32 [2, 256, 256], replicated, as said below
Outputs:
- eigenvectors: bfloat16 [2048, 2048], P('row', 'col')
The draws below stay inside these ranges and needn't reach their ends.
Inputs may be any that keep to these rules, and one draw needn't show every extreme that they name: `pole_order`: each value appears once. Distinct values; root j lies strictly between the poles at 2 * root_gap[j] and 2 * root_gap[j] + 2. `panel_factors`: upper triangular, with a diagonal between 2 and 4.
All inputs are finite; a program needn't handle non-finite values.
Results may differ from the reference program's by a relative error of at most 0.02.
Values may be sent and summed in bfloat16 or wider, within the bound.
No kernel may reach another device: no remote copies, remote signals or barrier semaphores. Data moves between devices by JAX's collectives and lax.ppermute only.
A program may use at most 64 MiB of HBM per device.

```python
import math
import jax
import jax.numpy as jnp
from jax import lax

K = 16384
EIG = 2048
PW = 256
PANELS = 2
NR = 2048
BLOCK = 128
N_ROW = 4
N_COL = 8


def shared_order(key):
    return jax.random.permutation(jax.random.fold_in(key, 31), K).astype(jnp.int32)


def draw_pole_order(key, part):
    return shared_order(key)


def draw_pole_weight(key, part):
    order = shared_order(key)
    place = order.astype(jnp.float32) / K
    ramp = 0.25 + 4.0 * place * place * place
    factor_key = jax.random.fold_in(key, 32)
    factor = jnp.exp(jax.random.uniform(factor_key, (K,), jnp.float32, math.log(0.7), math.log(1.4)))
    return (ramp * factor).astype(jnp.float32)


def draw_eigvecs(key, part):
    order = shared_order(key)
    place = order.astype(jnp.float32) / K
    freq = jax.random.uniform(jax.random.fold_in(key, 41), (NR, 1), jnp.float32, 0.5, 3.0)
    phase = jax.random.uniform(jax.random.fold_in(key, 42), (NR, 1), jnp.float32, 0.0, 1.0)
    wave = jnp.tanh(4.0 * jnp.sin(2.0 * math.pi * (freq * place[None, :] + phase)))
    spread = jax.random.uniform(jax.random.fold_in(key, 43), (NR, K), jnp.float32, 0.0, 1.0)
    magnitude = 0.5 + spread
    return (wave * magnitude * K ** (-0.5)).astype(jnp.bfloat16)


def draw_root_gap(key, part):
    first_key = jax.random.fold_in(key, 11)
    second_key = jax.random.fold_in(key, 12)
    lowest = K // 16
    highest = K - K // 16 - 2
    inner = jax.random.permutation(first_key, highest - lowest - 1)[:EIG - 2] + lowest + 1
    values = jnp.concatenate([jnp.array([lowest, highest], dtype=jnp.int32), inner.astype(jnp.int32)])
    return jax.random.permutation(second_key, values).astype(jnp.int32)


def draw_panel_factors(key, part):
    first_key = jax.random.fold_in(key, 21)
    second_key = jax.random.fold_in(key, 22)
    diagonal = jax.random.uniform(first_key, (PANELS, PW), jnp.float32, 2.0, 4.0)
    upper = jnp.clip(jax.random.normal(second_key, (PANELS, PW, PW), jnp.float32), -4.0, 4.0)
    upper = jnp.triu(upper * (1.5 / PW ** 0.5), 1)
    eye_table = jnp.eye(PW, dtype=jnp.float32)
    return (upper + diagonal[:, :, None] * eye_table[None, :, :]).astype(jnp.float32)


def levels(rng, dims, shards, least, high):
    gain = 1.0
    for axis_at, parts in shards:
        heights = jax.random.uniform(jax.random.fold_in(jax.random.fold_in(rng, 6), axis_at), (parts,), jnp.float32, least / len(shards), high / len(shards))
        gain = gain * jnp.repeat(jnp.exp(heights), dims[axis_at] // parts).reshape((-1,) + (1,) * (len(dims) - 1 - axis_at))
    return gain


def bell_draw(own_key, shape, width, limit, split=(), kind=jnp.bfloat16):
    values = width * jax.random.normal(own_key, shape, jnp.float32)
    if split:
        values = values * levels(own_key, shape, split, -0.22, 0.18)
    return jnp.clip(values, -limit, limit).astype(kind)


def setup_inputs(seed: int = 0) -> dict:
    seeds = jax.random.split(jax.random.key(seed), 9)
    eigvecs = draw_eigvecs(jax.random.fold_in(seeds[8], 71), 0)
    pole_order = draw_pole_order(jax.random.fold_in(seeds[8], 71), 0)
    pole_weight = draw_pole_weight(jax.random.fold_in(seeds[8], 71), 0)
    root_gap = draw_root_gap(jax.random.fold_in(seeds[8], 71), 0)
    root_shift = jnp.clip(jax.random.uniform(seeds[4], (EIG,), jnp.float32, -0.25, 0.25), -0.25, 0.25)
    column_weight = jnp.clip(jnp.exp(jax.random.uniform(seeds[5], (EIG,), jnp.float32, math.log(4.0), math.log(40.0))), 4.0, 40.0)
    panel_vectors = bell_draw(seeds[6], (PANELS, NR, PW), NR ** -0.5, 0.125, ((1, 4),))
    panel_factors = draw_panel_factors(jax.random.fold_in(seeds[8], 71), 0)
    return {"eigvecs": eigvecs, "pole_order": pole_order, "pole_weight": pole_weight, "root_gap": root_gap, "root_shift": root_shift, "column_weight": column_weight, "panel_vectors": panel_vectors, "panel_factors": panel_factors}


def cauchy_block(pole_slice, weight_slice, root_gap, root_shift, column_weight):
    pole_values = 2.0 * pole_slice.astype(jnp.float32)
    root_values = 2.0 * root_gap.astype(jnp.float32) + 1.0 + root_shift
    numer = pole_weight_outer(weight_slice, column_weight)
    return (numer / (pole_values[:, None] - root_values[None, :])).astype(jnp.bfloat16)


def pole_weight_outer(weight_slice, column_weight):
    return weight_slice[:, None] * column_weight[None, :]


def reference(eigvecs, pole_order, pole_weight, root_gap, root_shift, column_weight, panel_vectors, panel_factors):
    width_dev = K // N_COL

    def add_block(running, block_index):
        first_pole = (block_index * width_dev).astype(jnp.int32)
        rows_slice = lax.dynamic_slice_in_dim(eigvecs, first_pole, width_dev, 1)
        pole_slice = lax.dynamic_slice_in_dim(pole_order, first_pole, width_dev, 0)
        weight_slice = lax.dynamic_slice_in_dim(pole_weight, first_pole, width_dev, 0)
        matrix = cauchy_block(pole_slice, weight_slice, root_gap, root_shift, column_weight)
        partial_value = jnp.dot(rows_slice, matrix, preferred_element_type=jnp.float32).astype(jnp.bfloat16)
        partial_value = lax.optimization_barrier(partial_value)
        return running + partial_value.astype(jnp.float32), None

    start_sum = jnp.zeros((NR, EIG), jnp.float32)
    summed, unused = lax.scan(add_block, start_sum, jnp.arange(N_COL, dtype=jnp.int32))
    merged = summed.astype(jnp.bfloat16)
    cyclic = merged.reshape(N_ROW, N_ROW, BLOCK, EIG).transpose(1, 0, 2, 3).reshape(NR, EIG)
    current = cyclic.astype(jnp.float32)
    highest = lax.Precision.HIGHEST
    for panel_index in range(PANELS):
        vectors = panel_vectors[panel_index].astype(jnp.float32)
        project = jnp.einsum("rp,rc->pc", vectors, current, precision=highest)
        factored = jnp.dot(panel_factors[panel_index], project, precision=highest)
        current = current - jnp.dot(vectors, factored, precision=highest)
    return current.astype(jnp.bfloat16)
```

```python
import functools

import jax
import jax.numpy as jnp
from jax import lax
from jax.experimental import pallas as pl
from jax.experimental.pallas import tpu as pltpu
from jax.sharding import PartitionSpec as P

BF = jnp.bfloat16
F32 = jnp.float32
HIGHEST = lax.Precision.HIGHEST
MIB = 2**20


def bit_orders(size, first):
    bits = list(range(first, size.bit_length() - 1))
    half = len(bits) // 2
    return bits, bits[half:] + bits[:half]


def halving_codes(bits):
    if not bits:
        return [0]
    rest = halving_codes(bits[1:])
    return [(1 << bits[0]) | code for code in rest] + rest


def product_kernel(plan, width, depth, *refs):
    eig_hbm, order_hbm, weight_hbm, gap_hbm, shift_hbm, scale_hbm = refs[:6]
    outs = refs[6:6 + len(plan)]
    eig, order, weight, gap, shift, scale, eig_sem, small_sem = refs[6 + len(plan):]
    poles = eig.shape[1]
    small = [
        pltpu.make_async_copy(src, dst, small_sem.at[i])
        for i, (src, dst) in enumerate(
            [(order_hbm, order), (gap_hbm, gap), (shift_hbm, shift), (weight_hbm, weight), (scale_hbm, scale)]
        )
    ]
    pieces = range(0, poles, depth)
    large = [
        pltpu.make_async_copy(eig_hbm.at[:, k:k + depth], eig.at[:, k:k + depth], eig_sem.at[i])
        for i, k in enumerate(pieces)
    ]
    for copy in small + large:
        copy.start()
    me = lax.axis_index("col")
    even = lax.rem(me, 2) == 0
    for copy in small:
        copy.wait()
    pole_values = (2.0 * order[...].astype(F32)).reshape(1, poles)
    weights = weight[...].reshape(1, poles)
    first = True
    for out, codes in zip(outs, plan):
        for place, (even_code, odd_code) in enumerate(codes):
            start = pl.multiple_of(jnp.bitwise_xor(me, jnp.where(even, even_code, odd_code)) * width, width)
            roots = 2.0 * gap[pl.ds(start, width)].astype(F32) + 1.0 + shift[pl.ds(start, width)]
            roots = roots.reshape(1, width)
            roots = jnp.concatenate(
                [jnp.broadcast_to(roots[:, j:j + 128], (128, 128)).T for j in range(0, width, 128)], 0
            )
            total = None
            for i, k in enumerate(pieces):
                if first:
                    large[i].wait()
                gaps = pole_values[:, k:k + depth] - jnp.concatenate([roots] * (depth // 128), 1)
                matrix = (weights[:, k:k + depth] / gaps).astype(BF)
                term = lax.dot_general(
                    eig[:, k:k + depth], matrix, (((1,), (1,)), ((), ())), preferred_element_type=F32
                )
                total = term if total is None else total + term
            first = False
            out[:, place * width:(place + 1) * width] = (
                total * scale[pl.ds(start, width)].reshape(1, width)
            ).astype(BF)


def products(plan, parts, eigvecs, pole_order, pole_weight, root_gap, root_shift, column_weight):
    rows, poles = eigvecs.shape
    roots = root_gap.shape[0]
    width = roots // parts
    if width % 128 or poles % 1024:
        me = lax.axis_index("col")
        results = []
        for codes in plan:
            codes = jnp.array(codes, jnp.int32)
            places = jnp.bitwise_xor(me, jnp.where(me % 2 == 0, codes[:, 0], codes[:, 1]))
            pick = lambda v: v.reshape(parts, width)[places].reshape(-1)
            root_values = 2.0 * pick(root_gap).astype(F32) + 1.0 + pick(root_shift)
            numer = pole_weight[:, None] * pick(column_weight)[None, :]
            gaps = 2.0 * pole_order.astype(F32)[:, None] - root_values[None, :]
            matrix = (numer / gaps).astype(BF)
            results.append(jnp.dot(eigvecs, matrix, preferred_element_type=F32).astype(BF))
        return results
    depth = poles // 2
    count = sum(len(codes) for codes in plan)
    return pl.pallas_call(
        functools.partial(product_kernel, plan, width, depth),
        in_specs=[pl.BlockSpec(memory_space=pl.ANY)] * 6,
        out_specs=[pl.BlockSpec(memory_space=pltpu.VMEM)] * len(plan),
        out_shape=[jax.ShapeDtypeStruct((rows, width * len(codes)), BF) for codes in plan],
        scratch_shapes=[
            pltpu.VMEM((rows, poles), BF),
            pltpu.VMEM((poles,), jnp.int32),
            pltpu.VMEM((poles,), F32),
            pltpu.VMEM((roots,), jnp.int32),
            pltpu.VMEM((roots,), F32),
            pltpu.VMEM((roots,), F32),
            pltpu.SemaphoreType.DMA((2,)),
            pltpu.SemaphoreType.DMA((5,)),
        ],
        compiler_params=pltpu.CompilerParams(vmem_limit_bytes=60 * MIB),
        cost_estimate=pl.CostEstimate(
            flops=2 * rows * poles * width * count, bytes_accessed=3 * MIB, transcendentals=0
        ),
    )(eigvecs, pole_order, pole_weight, root_gap, root_shift, column_weight)


def shards(
    n_row,
    n_col,
    eigvecs,
    pole_order,
    pole_weight,
    root_gap,
    root_shift,
    column_weight,
    panel_vectors,
    panel_factors,
):
    col_orders = bit_orders(n_col, 1)
    row_orders = bit_orders(n_row, 0)
    row = lax.axis_index("row")
    core = lax.axis_index("col") % 2

    def swap_cores(value):
        return lax.ppermute(value, "col", [(i, i ^ 1) for i in range(n_col)])

    def swap_col(value, stage):
        return lax.ppermute(value, "col", [(i, i ^ (1 << col_orders[i % 2][stage])) for i in range(n_col)])

    def swap_row(value, stage):
        pairs = [
            (r * n_col + c, (r ^ (1 << row_orders[c % 2][stage])) * n_col + c)
            for r in range(n_row)
            for c in range(n_col)
        ]
        return lax.ppermute(value, ("row", "col"), pairs)

    def by_core(pair):
        return jnp.where(core == 0, pair[0], pair[1])

    def add(left, right):
        return left.astype(F32) + right.astype(F32)

    def pick_code(codes):
        return by_core((jnp.array(codes[0], jnp.int32), jnp.array(codes[1], jnp.int32)))

    row_codes = [halving_codes(order) for order in row_orders]

    def to_blocks(value):
        blocks = value.reshape((n_row, value.shape[0] // n_row) + value.shape[1:])
        return blocks[jnp.bitwise_xor(row, pick_code(row_codes))]

    def from_blocks(blocks, codes):
        inverse = [[list(c).index(d) for d in range(n_row)] for c in codes]
        places = pick_code(inverse)[jnp.bitwise_xor(row, jnp.arange(n_row, dtype=jnp.int32))]
        value = blocks[places]
        return value.reshape((-1,) + value.shape[2:])

    def source_codes():
        result = []
        for order in row_orders:
            codes = [0]
            for bit in order:
                codes = codes + [code | (1 << bit) for code in codes]
            result.append(codes)
        return result

    def exchange_step(blocks, stage, extra=None):
        half = blocks.shape[1] // 2
        sent, kept = blocks[:, :half], blocks[:, half:]
        shape = sent.shape
        if extra is None:
            got = swap_row(sent, stage)
            return jnp.concatenate([kept, got], 0), None
        flat = sent.reshape(-1, shape[-1])
        message = jnp.concatenate([extra, flat], 0)
        got = swap_row(message, stage)
        return (
            jnp.concatenate([kept, got[extra.shape[0]:].reshape(shape)], 0),
            got[:extra.shape[0]],
        )

    own = [halving_codes(order) for order in col_orders]
    own_codes = list(zip(own[0], own[1]))
    other_codes = [(1 ^ b, 1 ^ a) for a, b in own_codes]
    half = len(own_codes) // 2
    inputs = (eigvecs, pole_order, pole_weight, root_gap, root_shift, column_weight)
    other_sent, own_sent = products([other_codes[:half], own_codes[:half]], n_col, *inputs)
    got_sent = swap_cores(other_sent)
    sent = add(own_sent, got_sent).astype(BF)
    got = swap_col(sent, 0)
    other_kept, own_kept = products([other_codes[half:], own_codes[half:]], n_col, *inputs)
    got_kept = swap_cores(other_kept)

    mine = panel_vectors[core]
    panel_width = panel_vectors.shape[2]
    near = panel_width // 2
    first_vectors = panel_vectors[0]
    second_vectors = panel_vectors[1]
    second_half = lax.dynamic_slice_in_dim(second_vectors, core * near, near, 1)
    correlation = jnp.einsum("rp,rq->pq", second_half, first_vectors, preferred_element_type=F32)
    blocks = to_blocks(mine)[None]
    for stage in range(len(row_orders[0])):
        blocks, extra = exchange_step(blocks, stage, correlation.astype(BF))
        correlation = add(correlation, extra)
    mine_merged = from_blocks(blocks[:, 0], source_codes())
    both = swap_cores(jnp.concatenate([mine_merged, correlation.astype(BF)], 0))
    other_merged, other_correlation = both[:mine_merged.shape[0]], both[mine_merged.shape[0]:].astype(F32)
    correlation = jnp.where(
        core == 0,
        jnp.concatenate([correlation, other_correlation], 0),
        jnp.concatenate([other_correlation, correlation], 0),
    )
    across = jnp.dot(panel_factors[1], correlation, precision=HIGHEST)
    across = first_vectors.astype(F32) - jnp.dot(second_vectors.astype(F32), across, precision=HIGHEST)
    update_first = jnp.dot(across, panel_factors[0], precision=HIGHEST).astype(BF)
    update_second = jnp.dot(second_vectors.astype(F32), panel_factors[1], precision=HIGHEST).astype(BF)
    update = jnp.concatenate(
        [by_core((update_first, update_second)), by_core((update_second, update_first))], 1
    )
    merged_vectors = jnp.concatenate([mine_merged, other_merged], 1)

    kept = add(own_kept, got_kept)
    current = kept + got.astype(F32)
    for stage in range(1, len(col_orders[0])):
        middle = current.shape[1] // 2
        got = swap_col(current[:, :middle].astype(BF), stage)
        current = current[:, middle:] + got.astype(F32)
    merged = current.astype(BF)

    project = jnp.einsum("rp,rc->pc", merged_vectors, merged, preferred_element_type=F32)
    blocks = to_blocks(merged)[None]
    stages = len(row_orders[0])
    row_bits = [jnp.bitwise_and(lax.shift_right_logical(row, pick_code([[o[s]] for o in row_orders])[0]), 1) for s in range(stages)]
    for stage in range(stages - 1):
        middle = project.shape[0] // 2
        kept = lax.dynamic_slice_in_dim(project, row_bits[stage] * middle, middle, 0)
        sent = lax.dynamic_slice_in_dim(project, (1 - row_bits[stage]) * middle, middle, 0)
        blocks, extra = exchange_step(blocks, stage, sent.astype(BF))
        project = add(kept, extra)
    blocks, extra = exchange_step(blocks, stages - 1, project.astype(BF))
    project = add(project, extra).astype(BF)
    cyclic = from_blocks(blocks[:, 0], source_codes())
    for stage in reversed(range(stages - 1)):
        extra = swap_row(project, stage)
        project = jnp.where(
            row_bits[stage] == 0,
            jnp.concatenate([project, extra], 0),
            jnp.concatenate([extra, project], 0),
        )
    return (cyclic.astype(F32) - jnp.dot(update, project, preferred_element_type=F32)).astype(BF)


def solution(mesh):
    return jax.shard_map(
        functools.partial(shards, mesh.shape["row"], mesh.shape["col"]),
        mesh=mesh,
        in_specs=(P("row", "col"), P("col"), P("col"), P(), P(), P(), P(None, "row", None), P()),
        out_specs=P("row", "col"),
        check_vma=False,
    )
```

```python
import functools

import jax
import jax.numpy as jnp
from jax import lax
from jax.experimental import pallas as pl
from jax.experimental.pallas import tpu as pltpu
from jax.sharding import PartitionSpec as P

BF = jnp.bfloat16
F32 = jnp.float32
HIGHEST = lax.Precision.HIGHEST
MIB = 2**20
CHUNKS = 1


def bit_orders(size, first):
    bits = list(range(first, size.bit_length() - 1))
    half = len(bits) // 2
    return bits, bits[half:] + bits[:half]


def target_codes(bits):
    if not bits:
        return [0]
    rest = target_codes(bits[1:])
    return rest + [(1 << bits[0]) | code for code in rest]


def source_codes(bits):
    codes = [0]
    for bit in bits:
        codes = codes + [(1 << bit) | code for code in codes]
    return codes


def other_places(orders):
    even, odd = [target_codes(order) for order in orders]
    places = [even.index(code) for code in odd]
    assert places == [odd.index(code) for code in even]
    return places


def is_even():
    return lax.rem(lax.axis_index("col"), 2) == 0


def select_code(even, pair):
    return pair[0] if pair[0] == pair[1] else jnp.where(even, pair[0], pair[1])


def row_bit(row_orders, stage):
    shift = select_code(is_even(), (row_orders[0][stage], row_orders[1][stage]))
    return jnp.bitwise_and(lax.shift_right_logical(lax.axis_index("row"), shift), 1) == 0


def swap_groups(value, axis, row_orders):
    size = value.shape[axis]
    for stage in range(len(row_orders[0]) - 1):
        step = size >> (stage + 1)
        pieces = [lax.slice_in_dim(value, i, i + step, axis=axis) for i in range(0, size, step)]
        flipped = jnp.concatenate([pieces[i ^ 1] for i in range(len(pieces))], axis)
        value = jnp.where(row_bit(row_orders, stage), value, flipped)
    return value


def local(fn, outs, values, after=()):
    outs = [jax.ShapeDtypeStruct(shape, dtype) for shape, dtype in outs]
    if any(v.shape[-1] % 128 or v.shape[-2] % 16 for v in list(values) + outs):
        return list(fn(*values))

    def kernel(*refs):
        ins = refs[:len(values)]
        results = fn(*[ref[...] for ref in ins])
        for ref, result in zip(refs[len(values) + len(after):], results):
            ref[...] = result

    return list(
        pl.pallas_call(
            kernel,
            in_specs=[pl.BlockSpec(memory_space=pltpu.VMEM)] * len(values)
            + [pl.BlockSpec(memory_space=pl.ANY)] * len(after),
            out_specs=[pl.BlockSpec(memory_space=pltpu.VMEM)] * len(outs),
            out_shape=[pltpu.VMEM(o.shape, o.dtype) for o in outs],
            compiler_params=pltpu.CompilerParams(vmem_limit_bytes=16 * MIB),
            cost_estimate=pl.CostEstimate(flops=1, bytes_accessed=1, transcendentals=0),
        )(*[pltpu.with_memory_space_constraint(v, pltpu.VMEM) for v in values], *after)
    )


def product_kernel(plan, row_codes, row_places, width, depth, n_after, *refs):
    eig_hbm, order_hbm, weight_hbm, gap_hbm, shift_hbm, scale_hbm = refs[:6]
    refs = refs[6 + n_after:]
    outs = refs[:len(plan)]
    eig, order, weight, gap, shift, scale, eig_sem, small_sem = refs[len(plan):]
    rows, poles = eig.shape
    me = lax.axis_index("col")
    row = lax.axis_index("row")
    even = is_even()
    small = [
        pltpu.make_async_copy(src, dst, small_sem.at[i])
        for i, (src, dst) in enumerate(
            [(order_hbm, order), (gap_hbm, gap), (shift_hbm, shift), (weight_hbm, weight), (scale_hbm, scale)]
        )
    ]
    pieces = range(0, poles, depth)
    block = rows // len(row_codes)
    large = []
    for i, k in enumerate(pieces):
        group = []
        for place, pair in enumerate(row_codes):
            start = pl.multiple_of(jnp.bitwise_xor(row, select_code(even, pair)) * block, block)
            group.append(
                pltpu.make_async_copy(
                    eig_hbm.at[pl.ds(start, block), k:k + depth],
                    eig.at[place * block:(place + 1) * block, k:k + depth],
                    eig_sem.at[i, place],
                )
            )
        large.append(group)
    for copy in small + sum(large, []):
        copy.start()
    for copy in small:
        copy.wait()
    pole_values = (2.0 * order[...].astype(F32)).reshape(1, poles)
    weights = weight[...].reshape(1, poles)
    first = True
    for out, codes, places in zip(outs, plan, row_places):
        piece = width // CHUNKS
        for place, pair in enumerate(codes):
            start = pl.multiple_of(jnp.bitwise_xor(me, select_code(even, pair)) * width, width)
            roots = 2.0 * gap[pl.ds(start, width)].astype(F32) + 1.0 + shift[pl.ds(start, width)]
            roots = roots.reshape(1, width)
            roots = jnp.concatenate(
                [jnp.broadcast_to(roots[:, j:j + 128], (128, 128)).T for j in range(0, width, 128)], 0
            )
            total = None
            for i, k in enumerate(pieces):
                if first:
                    for copy in large[i]:
                        copy.wait()
                gaps = pole_values[:, k:k + depth] - jnp.concatenate([roots] * (depth // 128), 1)
                matrix = (weights[:, k:k + depth] / gaps).astype(BF)
                term = lax.dot_general(
                    eig[:, k:k + depth], matrix, (((1,), (1,)), ((), ())), preferred_element_type=F32
                )
                total = term if total is None else total + term
            first = False
            total = (total * scale[pl.ds(start, width)].reshape(1, width)).astype(BF)
            for chunk in range(CHUNKS):
                at = (chunk * len(codes) + place) * piece
                columns = total[:, chunk * piece:(chunk + 1) * piece]
                for target, source in enumerate(places):
                    out[target * block:(target + 1) * block, at:at + piece] = columns[
                        source * block:(source + 1) * block
                    ]


def products(plan, row_codes, row_places, parts, operands, after=()):
    eigvecs, pole_order, pole_weight, root_gap, root_shift, column_weight = operands
    rows, poles = eigvecs.shape
    roots = root_gap.shape[0]
    width = roots // parts
    if width % (128 * CHUNKS) or poles % 256:
        me = lax.axis_index("col")
        numbers = lambda pairs: jnp.array([[a, b] for a, b in pairs], jnp.int32)
        places = numbers(row_codes)
        places = jnp.bitwise_xor(lax.axis_index("row"), jnp.where(is_even(), places[:, 0], places[:, 1]))
        ordered = eigvecs.reshape(len(row_codes), -1, poles)[places].reshape(rows, poles)
        results = []
        for codes, row_place in zip(plan, row_places):
            places = numbers(codes)
            places = jnp.bitwise_xor(me, jnp.where(is_even(), places[:, 0], places[:, 1]))
            pick = lambda v: v.reshape(parts, CHUNKS, -1)[places].transpose(1, 0, 2).reshape(-1)
            root_values = 2.0 * pick(root_gap).astype(F32) + 1.0 + pick(root_shift)
            numer = pole_weight[:, None] * pick(column_weight)[None, :]
            gaps = 2.0 * pole_order.astype(F32)[:, None] - root_values[None, :]
            matrix = (numer / gaps).astype(BF)
            result = jnp.dot(ordered, matrix, preferred_element_type=F32).astype(BF)
            result = result.reshape(len(row_codes), -1, result.shape[1])
            results.append(jnp.concatenate([result[i] for i in row_place], 0))
        return results
    depth = poles // 2
    return pl.pallas_call(
        functools.partial(product_kernel, plan, row_codes, row_places, width, depth, len(after)),
        in_specs=[pl.BlockSpec(memory_space=pl.ANY)] * (6 + len(after)),
        out_specs=[pl.BlockSpec(memory_space=pltpu.VMEM)] * len(plan),
        out_shape=[pltpu.VMEM((rows, width * len(codes)), BF) for codes in plan],
        scratch_shapes=[
            pltpu.VMEM((rows, poles), BF),
            pltpu.VMEM((poles,), jnp.int32),
            pltpu.VMEM((poles,), F32),
            pltpu.VMEM((roots,), jnp.int32),
            pltpu.VMEM((roots,), F32),
            pltpu.VMEM((roots,), F32),
            pltpu.SemaphoreType.DMA((2, len(row_codes))),
            pltpu.SemaphoreType.DMA((5,)),
        ],
        compiler_params=pltpu.CompilerParams(vmem_limit_bytes=24 * MIB),
        cost_estimate=pl.CostEstimate(flops=1, bytes_accessed=1, transcendentals=0),
    )(*[pltpu.with_memory_space_constraint(operand, pltpu.HBM) for operand in operands], *after)


def panel_kernel(row_orders, blocks, near, *refs):
    panel, vectors_out, correlation_out = refs[:3]
    mine_out = refs[3:]
    even = is_even()
    row = lax.axis_index("row")
    block = panel.shape[1] // blocks
    sources = list(zip(*[source_codes(order) for order in row_orders]))
    targets = list(zip(*[target_codes(order) for order in row_orders]))
    at = lambda pair: pl.ds(pl.multiple_of(jnp.bitwise_xor(row, select_code(even, pair)) * block, block), block)
    for place, pair in enumerate(sources):
        vectors_out[0, place * block:(place + 1) * block] = panel[0, at(pair)]
        vectors_out[1, place * block:(place + 1) * block] = panel[1, at(pair)]
    core = jnp.where(even, 0, 1)
    for out, pair in zip(mine_out, targets):
        out[...] = panel[core, at(pair)]
    half = panel[1, :, pl.ds(pl.multiple_of(core * near, near), near)]
    correlation_out[...] = lax.dot_general(
        half, panel[0], (((0,), (0,)), ((), ())), preferred_element_type=F32
    ).astype(BF)


def panel_blocks(row_orders, panel_vectors):
    panels, rows, width = panel_vectors.shape
    blocks = 1 << len(row_orders[0])
    near = width // 2
    shapes = [(panels, rows, width), (near, width)] + [(rows // blocks, width)] * blocks
    return pl.pallas_call(
        functools.partial(panel_kernel, row_orders, blocks, near),
        in_specs=[pl.BlockSpec(memory_space=pltpu.VMEM)],
        out_specs=[pl.BlockSpec(memory_space=pltpu.VMEM)] * len(shapes),
        out_shape=[pltpu.VMEM(shape, BF) for shape in shapes],
        compiler_params=pltpu.CompilerParams(vmem_limit_bytes=16 * MIB),
        cost_estimate=pl.CostEstimate(flops=1, bytes_accessed=1, transcendentals=0),
    )(pltpu.with_memory_space_constraint(panel_vectors, pltpu.VMEM))


def finish_kernel(row_orders, blocks, refs_in, *refs):
    totals, update, project, out_hbm, result, sem = refs
    rows = totals.shape[0]
    block = rows // blocks
    even = is_even()
    row = lax.axis_index("row")
    sources = list(zip(*[source_codes(order) for order in row_orders]))
    value = totals[...] - jnp.dot(update[...], project[...], preferred_element_type=F32)
    result[...] = value.astype(BF)
    copies = []
    for place, pair in enumerate(sources):
        start = pl.multiple_of(jnp.bitwise_xor(row, select_code(even, pair)) * block, block)
        copies.append(
            pltpu.make_async_copy(
                result.at[place * block:(place + 1) * block], out_hbm.at[pl.ds(start, block)], sem.at[place]
            )
        )
    for copy in copies:
        copy.start()
    for copy in copies:
        copy.wait()


def finish(row_orders, totals, update, project):
    rows, width = totals.shape
    blocks = 1 << len(row_orders[0])
    if width % 128:
        result = (totals - jnp.dot(update, project, preferred_element_type=F32)).astype(BF)
        result = result.reshape(blocks, -1, width)
        sources = [source_codes(order) for order in row_orders]
        ordered = [[s.index(code) for code in range(blocks)] for s in sources]
        places = jnp.where(is_even(), jnp.array(ordered[0]), jnp.array(ordered[1]))
        return result[places[jnp.bitwise_xor(lax.axis_index("row"), jnp.arange(blocks))]].reshape(rows, width)
    return pl.pallas_call(
        functools.partial(finish_kernel, row_orders, blocks, None),
        in_specs=[pl.BlockSpec(memory_space=pltpu.VMEM)] * 3,
        out_specs=pl.BlockSpec(memory_space=pl.ANY),
        out_shape=jax.ShapeDtypeStruct((rows, width), BF),
        scratch_shapes=[pltpu.VMEM((rows, width), BF), pltpu.SemaphoreType.DMA((blocks,))],
        compiler_params=pltpu.CompilerParams(vmem_limit_bytes=16 * MIB),
        cost_estimate=pl.CostEstimate(flops=1, bytes_accessed=1, transcendentals=0),
    )(*[pltpu.with_memory_space_constraint(v, pltpu.VMEM) for v in (totals, update, project)])


def shards(
    n_row,
    n_col,
    eigvecs,
    pole_order,
    pole_weight,
    root_gap,
    root_shift,
    column_weight,
    panel_vectors,
    panel_factors,
):
    col_orders = bit_orders(n_col, 1)
    row_orders = bit_orders(n_row, 0)
    col_stages = len(col_orders[0])
    row_stages = len(row_orders[0])
    rows = eigvecs.shape[0]
    block = rows // n_row
    panel_width = panel_vectors.shape[2]
    near = panel_width // 2

    def swap_cores(value):
        return lax.ppermute(value, "col", [(i, i ^ 1) for i in range(n_col)])

    def swap_col(value, stage):
        return lax.ppermute(value, "col", [(i, i ^ (1 << col_orders[i % 2][stage])) for i in range(n_col)])

    def swap_row(value, stage):
        pairs = [
            (r * n_col + c, (r ^ (1 << row_orders[c % 2][stage])) * n_col + c)
            for r in range(n_row)
            for c in range(n_col)
        ]
        return lax.ppermute(value, ("row", "col"), pairs)

    def split_targets(blocks):
        sources, targets = blocks
        count = sum(s.shape[0] for s in sources) // (targets * block)
        kept, sent = [], []
        for source in sources:
            for i in range(0, source.shape[0], targets * block):
                middle = i + targets * block // 2
                kept.append(source[i:middle])
                sent.append(source[middle:i + targets * block])
        return jnp.concatenate(kept, 0), jnp.concatenate(sent, 0)

    targets = list(zip(*[target_codes(order) for order in row_orders]))
    own_codes = list(zip(*[target_codes(order) for order in col_orders]))
    other_codes = [(1 ^ odd, 1 ^ even) for even, odd in own_codes]
    half = len(own_codes) // 2
    operands = (eigvecs, pole_order, pole_weight, root_gap, root_shift, column_weight)
    other_rows = other_places(row_orders)
    row_places = [other_rows, list(range(n_row))]
    other_sent, own_sent = products(
        [other_codes[half:], own_codes[half:]], targets, row_places, n_col, operands
    )
    got_sent = swap_cores(other_sent)
    (sent,) = local(
        lambda a, b: [(a.astype(F32) + b.astype(F32)).astype(BF)], [(own_sent.shape, BF)], [own_sent, got_sent]
    )
    got = swap_col(sent, 0)

    vectors, correlation, *mine = panel_blocks(row_orders, panel_vectors)
    codes = list(zip(*[target_codes(order) for order in row_orders]))[1:]

    def send_to(value, pair):
        pairs = [(r * n_col + c, (r ^ pair[c % 2]) * n_col + c) for r in range(n_row) for c in range(n_col)]
        return lax.ppermute(value, ("row", "col"), pairs)

    panel_got = [send_to(message, pair) for message, pair in zip(mine[1:], codes)]
    correlation_got = [send_to(correlation, pair) for pair in codes]
    other_kept, own_kept = products(
        [other_codes[:half], own_codes[:half]], targets, row_places, n_col, operands, after=(sent, vectors)
    )
    got_kept = swap_cores(other_kept)

    piece = own_kept.shape[1] // 2 if col_stages > 1 else own_kept.shape[1]

    (current,) = local(
        lambda kept, got: [kept.astype(F32) + got.astype(F32)], [(own_kept.shape, F32)], [own_kept, got]
    )

    def first_sum(current, got):
        total = current + got.astype(F32)
        return total[:, :piece], total[:, piece:].astype(BF)

    current, sent = local(first_sum, [((rows, piece), F32), ((rows, piece), BF)], [current, got_kept])
    for stage in range(1, col_stages):
        got = swap_col(sent, stage)
        if stage < col_stages - 1:
            piece = piece // 2

            def next_sum(current, got, piece=piece):
                total = current + got.astype(F32)
                return total[:, :piece], total[:, piece:].astype(BF)

            current, sent = local(next_sum, [((rows, piece), F32), ((rows, piece), BF)], [current, got])

    mine_all, mine_sent = local(
        lambda *parts: [jnp.concatenate(parts, 0), jnp.concatenate([parts[i] for i in other_rows], 0)],
        [((rows, panel_width), BF)] * 2,
        mine[:1] + panel_got,
        after=(sent,),
    )
    other_all = swap_cores(mine_sent)

    width = piece

    (merged,) = local(
        lambda current, got: [(current + got.astype(F32)).astype(BF)], [((rows, width), BF)], [current, got]
    )

    def projections(merged, mine_all, other_all):
        dims = (((0,), (0,)), ((), ()))
        project = jnp.concatenate(
            [
                lax.dot_general(v, merged, dims, preferred_element_type=F32)
                for v in (mine_all, other_all)
            ],
            0,
        )
        project = swap_groups(project, 0, row_orders)
        middle = project.shape[0] // 2
        kept, moved = split_targets(([merged], n_row))
        if row_stages == 1:
            return project, project.astype(BF), kept, moved
        return project[:middle], project[middle:].astype(BF), kept, moved

    wide = 2 * panel_width
    kept_rows = wide // 2 if row_stages > 1 else wide
    project, project_sent, blocks, blocks_sent = local(
        projections,
        [((kept_rows, width), F32), ((kept_rows, width), BF), ((rows // 2, width), BF), ((rows // 2, width), BF)],
        [merged, mine_all, other_all],
    )
    project_got = swap_row(project_sent, 0)
    blocks_got = swap_row(blocks_sent, 0)

    def correlation_sum(*parts):
        return [sum(part.astype(F32) for part in parts).astype(BF)]

    (correlation,) = local(
        correlation_sum, [((near, panel_width), BF)], [correlation] + correlation_got, after=(merged,)
    )
    other_correlation = swap_cores(correlation)

    def update_factor(first_vectors, second_vectors, factor_first, factor_second, mine, other):
        mine, other = mine.astype(F32), other.astype(F32)
        even = is_even()
        correlation = jnp.concatenate([jnp.where(even, mine, other), jnp.where(even, other, mine)], 0)
        second_vectors = second_vectors.astype(F32)
        across = jnp.dot(factor_second, correlation, precision=HIGHEST, preferred_element_type=F32)
        across = jnp.dot(second_vectors, across, precision=HIGHEST, preferred_element_type=F32)
        across = first_vectors.astype(F32) - across
        first = jnp.dot(across, factor_first, precision=HIGHEST, preferred_element_type=F32)
        second = jnp.dot(second_vectors, factor_second, precision=HIGHEST, preferred_element_type=F32)
        update = jnp.concatenate([jnp.where(even, first, second), jnp.where(even, second, first)], 1)
        return [swap_groups(update, 1, row_orders).astype(BF)]

    (update,) = local(
        update_factor,
        [((rows, wide), BF)],
        [vectors[0], vectors[1], panel_factors[0], panel_factors[1], correlation, other_correlation],
        after=(project_sent,),
    )

    for stage in range(1, row_stages):
        last = stage == row_stages - 1
        middle = kept_rows if last else kept_rows // 2

        def next_project(project, got, last=last, middle=middle):
            total = project + got.astype(F32)
            if last:
                return total, total.astype(BF)
            return total[:middle], total[middle:].astype(BF)

        project, project_sent = local(
            next_project, [((middle, width), F32), ((middle, width), BF)], [project, project_got]
        )
        kept_rows = middle
        project_got = swap_row(project_sent, stage)
        blocks, blocks_sent = local(
            lambda blocks, got, targets=n_row >> stage: split_targets(([jnp.concatenate([blocks, got], 0)], targets)),
            [((rows // 2, width), BF), ((rows // 2, width), BF)],
            [blocks, blocks_got],
            after=(project_sent,),
        )
        blocks_got = swap_row(blocks_sent, stage)
    (project,) = local(
        lambda project, got: [(project + got.astype(F32)).astype(BF)], [((kept_rows, width), BF)], [project, project_got]
    )
    total = None
    start = 0
    for stage in reversed(range(row_stages - 1)):
        got = swap_row(project, stage)
        if total is None:
            (total,) = local(
                lambda blocks, blocks_got, update, project: [
                    jnp.concatenate([blocks, blocks_got], 0).astype(F32)
                    - jnp.dot(update[:, :project.shape[0]], project, preferred_element_type=F32)
                ],
                [((rows, width), F32)],
                [blocks, blocks_got, update, project],
                after=(project,),
            )
            start = project.shape[0]
        if stage > 0:
            project = jnp.concatenate([project, got], 0)
        else:
            rest = got if row_stages == 2 else jnp.concatenate([project, got], 0)[start:]
    return finish(row_orders, total, update[:, start:], rest)


def solution(mesh):
    return jax.shard_map(
        functools.partial(shards, mesh.shape["row"], mesh.shape["col"]),
        mesh=mesh,
        in_specs=(P("row", "col"), P("col"), P("col"), P(), P(), P(), P(None, "row", None), P()),
        out_specs=P("row", "col"),
        check_vma=False,
    )
```

```python
import functools

import jax
import jax.numpy as jnp
from jax import lax
from jax.experimental import pallas as pl
from jax.experimental.pallas import tpu as pltpu
from jax.sharding import PartitionSpec as P

BF = jnp.bfloat16
F32 = jnp.float32
HIGHEST = lax.Precision.HIGHEST
MIB = 2**20


def bit_orders(size, first):
    bits = list(range(first, size.bit_length() - 1))
    half = len(bits) // 2
    return bits, bits[half:] + bits[:half]


def target_codes(bits):
    if not bits:
        return [0]
    rest = target_codes(bits[1:])
    return rest + [(1 << bits[0]) | code for code in rest]


def source_codes(bits):
    codes = [0]
    for bit in bits:
        codes = codes + [(1 << bit) | code for code in codes]
    return codes


def is_even():
    return lax.rem(lax.axis_index("col"), 2) == 0


def select_code(even, pair):
    return pair[0] if pair[0] == pair[1] else jnp.where(even, pair[0], pair[1])


def row_bit(order, stage):
    return jnp.bitwise_and(lax.shift_right_logical(lax.axis_index("row"), order[stage]), 1) == 0


def swap_groups(value, axis, order):
    size = value.shape[axis]
    for stage in range(len(order) - 1):
        step = size >> (stage + 1)
        pieces = [lax.slice_in_dim(value, i, i + step, axis=axis) for i in range(0, size, step)]
        flipped = jnp.concatenate([pieces[i ^ 1] for i in range(len(pieces))], axis)
        value = jnp.where(row_bit(order, stage), value, flipped)
    return value


def local(fn, outs, values, after=()):
    outs = [jax.ShapeDtypeStruct(shape, dtype) for shape, dtype in outs]
    if any(v.shape[-1] % 128 or v.shape[-2] % 16 for v in list(values) + outs):
        return list(fn(*values))

    def kernel(*refs):
        ins = refs[:len(values)]
        results = fn(*[ref[...] for ref in ins])
        for ref, result in zip(refs[len(values) + len(after):], results):
            ref[...] = result

    return list(
        pl.pallas_call(
            kernel,
            in_specs=[pl.BlockSpec(memory_space=pltpu.VMEM)] * len(values)
            + [pl.BlockSpec(memory_space=pl.ANY)] * len(after),
            out_specs=[pl.BlockSpec(memory_space=pltpu.VMEM)] * len(outs),
            out_shape=[pltpu.VMEM(o.shape, o.dtype) for o in outs],
            compiler_params=pltpu.CompilerParams(vmem_limit_bytes=16 * MIB),
            cost_estimate=pl.CostEstimate(flops=1, bytes_accessed=1, transcendentals=0),
        )(*[pltpu.with_memory_space_constraint(v, pltpu.VMEM) for v in values], *after)
    )


def product_kernel(plan, width, depth, chunks, n_after, *refs):
    eig, pole_values, weights, roots, scale = refs[:5]
    outs = refs[5 + n_after:]
    rows, poles = eig.shape
    me = lax.axis_index("col")
    even = is_even()
    piece = width // chunks
    pole_values = pole_values[...]
    weights = weights[...]
    for entry, codes in enumerate(plan):
        for place, pair in enumerate(codes):
            at = pl.ds(pl.multiple_of(jnp.bitwise_xor(me, select_code(even, pair)) * width, width), width)
            near = roots[:, at]
            near = jnp.concatenate(
                [jnp.broadcast_to(near[:, j:j + 128], (128, 128)).T for j in range(0, width, 128)], 0
            )
            total = None
            for k in range(0, poles, depth):
                gaps = pole_values[:, k:k + depth] - jnp.concatenate([near] * (depth // 128), 1)
                matrix = (weights[:, k:k + depth] / gaps).astype(BF)
                term = lax.dot_general(
                    eig[:, k:k + depth], matrix, (((1,), (1,)), ((), ())), preferred_element_type=F32
                )
                total = term if total is None else total + term
            total = (total * scale[:, at]).astype(BF)
            for chunk in range(chunks):
                outs[entry * chunks + chunk][:, place * piece:(place + 1) * piece] = total[
                    :, chunk * piece:(chunk + 1) * piece
                ]


def plain_products(plan, row_codes, parts, chunks, operands):
    eigvecs, pole_order, pole_weight, root_gap, root_shift, column_weight = operands
    poles = eigvecs.shape[1]
    me = lax.axis_index("col")
    places = jnp.bitwise_xor(lax.axis_index("row"), jnp.array(row_codes, jnp.int32))
    ordered = eigvecs.reshape(len(row_codes), -1, poles)[places].reshape(eigvecs.shape)
    results = []
    for codes in plan:
        places = jnp.array([[a, b] for a, b in codes], jnp.int32)
        places = jnp.bitwise_xor(me, jnp.where(is_even(), places[:, 0], places[:, 1]))
        pick = lambda v: v.reshape(parts, chunks, -1)[places].transpose(1, 0, 2).reshape(-1)
        root_values = 2.0 * pick(root_gap).astype(F32) + 1.0 + pick(root_shift)
        numer = pole_weight[:, None] * pick(column_weight)[None, :]
        gaps = 2.0 * pole_order.astype(F32)[:, None] - root_values[None, :]
        result = jnp.dot(ordered, (numer / gaps).astype(BF), preferred_element_type=F32).astype(BF)
        results += jnp.split(result, chunks, 1)
    return results


def products(plan, *, row_codes, parts, chunks, operands, state, after=()):
    rows, poles = operands[0].shape
    width = operands[3].shape[0] // parts
    if state is None:
        return plain_products(plan, row_codes, parts, chunks, operands)
    outs = [pltpu.VMEM((rows, width // chunks * len(codes)), BF) for codes in plan for _ in range(chunks)]
    return pl.pallas_call(
        functools.partial(
            product_kernel, plan, width, poles // 2, chunks, len(after)
        ),
        in_specs=[pl.BlockSpec(memory_space=pltpu.VMEM)] * 5 + [pl.BlockSpec(memory_space=pl.ANY)] * len(after),
        out_specs=[pl.BlockSpec(memory_space=pltpu.VMEM)] * len(outs),
        out_shape=outs,
        compiler_params=pltpu.CompilerParams(vmem_limit_bytes=16 * MIB),
        cost_estimate=pl.CostEstimate(flops=1, bytes_accessed=1, transcendentals=0),
    )(*[pltpu.with_memory_space_constraint(operand, pltpu.VMEM) for operand in state], *after)


def panel_kernel(row_codes, row_orders, blocks, *refs):
    eig_hbm, panel_hbm, order_hbm, weight_hbm, gap_hbm, shift_hbm, scale_hbm = refs[:7]
    vectors_out, kept_out, message, correlation_out, eig, pole_values, weights, roots, scales = refs[7:16]
    panel, correlation, order, weight, gap, shift, scale, sem, eig_sem = refs[16:]
    even = is_even()
    row = lax.axis_index("row")
    block = panel.shape[1] // blocks
    targets = list(zip(*[target_codes(order) for order in row_orders]))
    at = lambda code: pl.ds(pl.multiple_of(jnp.bitwise_xor(row, code) * block, block), block)
    copies = [
        pltpu.make_async_copy(src, dst, sem.at[i])
        for i, (src, dst) in enumerate(
            [
                (panel_hbm, panel),
                (order_hbm, order),
                (weight_hbm, weight),
                (gap_hbm, gap),
                (shift_hbm, shift),
                (scale_hbm, scale),
            ]
        )
    ]
    for place, code in enumerate(row_codes):
        copies.append(
            pltpu.make_async_copy(
                eig_hbm.at[at(code)], eig.at[place * block:(place + 1) * block], eig_sem.at[place]
            )
        )
    for copy in copies:
        copy.start()
    for copy in copies[1:6]:
        copy.wait()
    pole_values[...] = (2.0 * order[...].astype(F32)).reshape(pole_values.shape)
    weights[...] = weight[...].reshape(weights.shape)
    roots[...] = (2.0 * gap[...].astype(F32) + 1.0 + shift[...]).reshape(roots.shape)
    scales[...] = scale[...].reshape(scales.shape)
    copies[0].wait()
    for code in range(blocks):
        vectors_out[0, code * block:(code + 1) * block] = panel[0, at(code)]
        vectors_out[1, code * block:(code + 1) * block] = panel[1, at(code)]
    core = jnp.where(even, 0, 1)
    correlation[...] = lax.dot_general(panel[1], panel[0], (((0,), (0,)), ((), ())), preferred_element_type=F32)
    near = correlation_out.shape[0]
    place = lax.shift_right_logical(lax.axis_index("col"), 1)
    part = correlation[pl.ds(pl.multiple_of(place * near, near), near)]
    correlation_out[...] = part
    message[:near] = part.astype(BF)
    for place, pair in enumerate(targets):
        value = panel[core, at(select_code(even, pair))]
        if place < blocks // 2:
            kept_out[place * block:(place + 1) * block] = value
        else:
            start = near + (place - blocks // 2) * block
            message[start:start + block] = value
    for copy in copies[6:]:
        copy.wait()


def panel_blocks(row_codes, row_orders, parts, panel_vectors, operands):
    panels, rows, width = panel_vectors.shape
    blocks = 1 << len(row_orders[0])
    near = width // parts
    poles, roots = operands[1].shape[0], operands[3].shape[0]
    eig_rows = operands[0].shape[0]
    outs = [
        pltpu.VMEM((panels, rows, width), BF),
        pltpu.VMEM((rows // 2, width), BF),
        pltpu.VMEM((near + rows // 2, width), BF),
        pltpu.VMEM((near, width), F32),
        pltpu.VMEM((eig_rows, poles), BF),
        pltpu.VMEM((1, poles), F32),
        pltpu.VMEM((1, poles), F32),
        pltpu.VMEM((1, roots), F32),
        pltpu.VMEM((1, roots), F32),
    ]
    results = pl.pallas_call(
        functools.partial(panel_kernel, row_codes, row_orders, blocks),
        in_specs=[pl.BlockSpec(memory_space=pl.ANY)] * 7,
        out_specs=[pl.BlockSpec(memory_space=pltpu.VMEM)] * len(outs),
        out_shape=outs,
        scratch_shapes=[
            pltpu.VMEM((panels, rows, width), BF),
            pltpu.VMEM((width, width), F32),
            pltpu.VMEM((poles,), jnp.int32),
            pltpu.VMEM((poles,), F32),
            pltpu.VMEM((roots,), jnp.int32),
            pltpu.VMEM((roots,), F32),
            pltpu.VMEM((roots,), F32),
            pltpu.SemaphoreType.DMA((6,)),
            pltpu.SemaphoreType.DMA((blocks,)),
        ],
        compiler_params=pltpu.CompilerParams(vmem_limit_bytes=16 * MIB),
        cost_estimate=pl.CostEstimate(flops=1, bytes_accessed=1, transcendentals=0),
    )(*[pltpu.with_memory_space_constraint(v, pltpu.HBM) for v in (operands[0], panel_vectors, *operands[1:])])
    return results[:4], results[4:]


def finish_kernel(blocks, start, total, update, project, out_hbm, result, sem):
    block = total.shape[0] // blocks
    row = lax.axis_index("row")
    value = total[...] - jnp.dot(update[:, start:], project[...], preferred_element_type=F32)
    result[...] = value.astype(BF)
    copies = []
    for code in range(blocks):
        at = pl.multiple_of(jnp.bitwise_xor(row, code) * block, block)
        copies.append(
            pltpu.make_async_copy(
                result.at[code * block:(code + 1) * block], out_hbm.at[pl.ds(at, block)], sem.at[code]
            )
        )
        copies[-1].start()
    for copy in copies:
        copy.wait()


def finish(blocks, total, update, project, start):
    rows, width = total.shape
    if width % 128:
        result = (total - jnp.dot(update[:, start:], project, preferred_element_type=F32)).astype(BF)
        places = jnp.bitwise_xor(lax.axis_index("row"), jnp.arange(blocks))
        return result.reshape(blocks, -1, width)[places].reshape(rows, width)
    return pl.pallas_call(
        functools.partial(finish_kernel, blocks, start),
        in_specs=[pl.BlockSpec(memory_space=pltpu.VMEM)] * 3,
        out_specs=pl.BlockSpec(memory_space=pl.ANY),
        out_shape=jax.ShapeDtypeStruct((rows, width), BF),
        scratch_shapes=[pltpu.VMEM((rows, width), BF), pltpu.SemaphoreType.DMA((blocks,))],
        compiler_params=pltpu.CompilerParams(vmem_limit_bytes=16 * MIB),
        cost_estimate=pl.CostEstimate(flops=1, bytes_accessed=1, transcendentals=0),
    )(*[pltpu.with_memory_space_constraint(v, pltpu.VMEM) for v in (total, update, project)])


def split_dot(left, right):
    def parts(value):
        if value.dtype == BF:
            return [value]
        high = value.astype(BF)
        return [high, (value - high.astype(F32)).astype(BF)]

    total = None
    for i, a in enumerate(parts(left)):
        for j, b in enumerate(parts(right)):
            if i + j < 2:
                term = jnp.dot(a, b, preferred_element_type=F32)
                total = term if total is None else total + term
    return total


def shards(
    n_row,
    n_col,
    eigvecs,
    pole_order,
    pole_weight,
    root_gap,
    root_shift,
    column_weight,
    panel_vectors,
    panel_factors,
):
    col_orders = bit_orders(n_col, 1)
    row_orders = bit_orders(n_row, 0)
    col_stages = len(col_orders[0])
    row_stages = len(row_orders[0])
    rows = eigvecs.shape[0]
    block = rows // n_row
    panel_width = panel_vectors.shape[2]
    parts = n_col // 2
    near = panel_width // parts
    width = root_gap.shape[0] // n_col
    chunks = 2 if width % 256 == 0 else 1
    piece = width // chunks
    sum_order = row_orders[0]
    move_order = sum_order[::-1]

    def swap_cores(value):
        return lax.ppermute(value, "col", [(i, i ^ 1) for i in range(n_col)])

    def swap_col(value, stage):
        return lax.ppermute(value, "col", [(i, i ^ (1 << col_orders[i % 2][stage])) for i in range(n_col)])

    def swap_row(value, bits):
        pairs = [(r * n_col + c, (r ^ (1 << bits[c % 2])) * n_col + c) for r in range(n_row) for c in range(n_col)]
        return lax.ppermute(value, ("row", "col"), pairs)

    def split_targets(value, targets):
        step = targets * block
        kept = [value[i:i + step // 2] for i in range(0, value.shape[0], step)]
        sent = [value[i + step // 2:i + step] for i in range(0, value.shape[0], step)]
        return jnp.concatenate(kept, 0), jnp.concatenate(sent, 0)

    def pick_blocks(value, places):
        return jnp.concatenate([value[i * block:(i + 1) * block] for i in places], 0)

    targets = target_codes(move_order)
    own_codes = list(zip(*[target_codes(order) for order in col_orders]))
    other_codes = [(1 ^ odd, 1 ^ even) for even, odd in own_codes]
    half = len(own_codes) // 2
    operands = (eigvecs, pole_order, pole_weight, root_gap, root_shift, column_weight)
    (vectors, kept, message, correlation), state = panel_blocks(
        targets, row_orders, parts, panel_vectors, operands
    )
    if width % (128 * chunks) or eigvecs.shape[1] % 256:
        state = None
    multiply = functools.partial(
        products, row_codes=targets, parts=n_col, chunks=chunks, operands=operands, state=state
    )
    first = multiply([other_codes[half:], own_codes[half:]])
    other_sent, own_sent = first[:chunks], first[chunks:]
    got_sent = [swap_cores(value) for value in other_sent]
    other_kept = multiply([other_codes[:half]])
    got_kept = [swap_cores(value) for value in other_kept]
    long = half * piece
    sent = []
    for own, got in zip(own_sent, got_sent):
        (value,) = local(
            lambda own, got: [(own.astype(F32) + got.astype(F32)).astype(BF)],
            [((rows, long), BF)],
            [own, got],
            after=(other_kept[0], *sent),
        )
        sent.append(value)
    got = [swap_col(message, 0) for message in sent]
    own_kept = multiply([own_codes[:half]], after=(sent[0],))

    current = [[own, other, new] for own, other, new in zip(own_kept, got_kept, got)]
    for stage in range(1, col_stages):
        long //= 2

        def next_sums(*values, long=long):
            count = len(values) // chunks
            totals = [sum(v.astype(F32) for v in values[i:i + count]) for i in range(0, len(values), count)]
            out = jnp.concatenate([total[:, long:] for total in totals], 1).astype(BF)
            return *[total[:, :long] for total in totals], out

        *totals, col_message = local(
            next_sums,
            [((rows, long), F32)] * chunks + [((rows, chunks * long), BF)],
            sum(current, []),
        )
        if stage == 1:
            first_message = col_message
        got = swap_col(col_message, stage)
        current = [[total, got] for total in totals]
        if stage < col_stages - 1:
            current = [[total, got[:, i * long:(i + 1) * long]] for i, total in enumerate(totals)]

    for stage in range(row_stages):
        panel_got = swap_row(message, [order[stage] for order in row_orders])

        if stage < row_stages - 1:

            def next_panel(kept, correlation, got, targets=n_row >> (stage + 1)):
                correlation = correlation + got[:near].astype(F32)
                kept, moved = split_targets(jnp.concatenate([kept, got[near:]], 0), targets)
                return kept, jnp.concatenate([correlation.astype(BF), moved], 0), correlation

            kept, message, correlation = local(
                next_panel,
                [((rows // 2, panel_width), BF), ((near + rows // 2, panel_width), BF), ((near, panel_width), F32)],
                [kept, correlation, panel_got],
                after=(other_kept[0],),
            )
    panel_places = [[source_codes(order).index(code) for code in range(n_row)] for order in row_orders]

    first_rows = 3 * rows // 4

    def panel_done(kept, correlation, got):
        correlation = (correlation + got[:near].astype(F32)).astype(BF)
        value = jnp.concatenate([kept, got[near:]], 0)
        orders = [pick_blocks(value, places).astype(F32) for places in panel_places]
        value = jnp.where(is_even(), orders[0], orders[1]).astype(BF)
        return value, correlation, value[:first_rows], value[first_rows:]

    mine, correlation, *mine_sent = local(
        panel_done,
        [((r, panel_width), BF) for r in (rows, near, first_rows, rows - first_rows)],
        [kept, correlation, panel_got],
        after=(first_message,),
    )
    other = [swap_cores(value) for value in mine_sent]

    wide = 2 * panel_width
    summed = wide // 2 if row_stages > 1 else wide

    def projections(mine, *values):
        other, values = values[:2], values[2:]
        merged = jnp.concatenate(values[:chunks], 1) + jnp.concatenate(values[chunks:], 1).astype(F32)
        merged = merged.astype(BF)
        dims = (((0,), (0,)), ((), ()))
        project = jnp.concatenate(
            [
                lax.dot_general(pick_blocks(v, targets), merged, dims, preferred_element_type=F32)
                for v in (mine, jnp.concatenate(other, 0))
            ],
            0,
        )
        project = swap_groups(project, 0, sum_order)
        out = project if row_stages == 1 else project[summed:]
        return project[:summed], out.astype(BF), *split_targets(merged, n_row)

    shapes = lambda size: [((size, width), F32), ((size, width), BF)]
    halves = [((rows // 2, width), BF)] * 2
    last_got = [current[0][1]] if col_stages > 1 else [c[1] for c in current]
    project, message, blocks, moved = local(
        projections,
        shapes(summed) + halves,
        [mine, *other, *[c[0] for c in current], *last_got],
    )
    project_got = swap_row(message, [sum_order[0]] * 2)
    blocks_got = swap_row(moved, [move_order[0]] * 2)

    def join(mine, got, stage):
        shift = select_code(is_even(), (col_orders[0][stage], col_orders[1][stage]))
        low = jnp.bitwise_and(lax.shift_right_logical(lax.axis_index("col"), shift), 1) == 0
        mine, got = mine.astype(F32), got.astype(F32)
        return jnp.concatenate([jnp.where(low, mine, got), jnp.where(low, got, mine)], 0)

    joined = near
    for stage in range(col_stages - 1):
        joined *= 2
        (correlation,) = local(
            lambda mine, got, stage=stage: [join(mine, got, stage).astype(BF)],
            [((joined, panel_width), BF)],
            [correlation, swap_col(correlation, stage)],
            after=(message,),
        )
    other_correlation = swap_col(correlation, col_stages - 1)
    part_orders = [source_codes([bit - 1 for bit in order]) for order in col_orders]
    part_orders = [[order.index(part) for part in range(parts)] for order in part_orders]

    def update_factor(vectors, factors, mine, other):
        even = is_even()
        correlation = join(mine, other, col_stages - 1)
        ordered = [
            jnp.concatenate([correlation[i * near:(i + 1) * near] for i in order], 0) for order in part_orders
        ]
        correlation = jnp.where(even, ordered[0], ordered[1]).astype(BF)
        across = split_dot(vectors[1], split_dot(factors[1], correlation))
        first = split_dot(vectors[0].astype(F32) - across, factors[0])
        second = split_dot(vectors[1], factors[1])
        update = jnp.concatenate([jnp.where(even, first, second), jnp.where(even, second, first)], 1)
        return [swap_groups(update, 1, sum_order).astype(BF)]

    for stage in range(1, row_stages):
        last = stage == row_stages - 1
        size = summed if last else summed // 2

        def next_project(project, got, last=last, size=size):
            total = project + got.astype(F32)
            return total[:size], (total if last else total[size:]).astype(BF)

        project, message = local(
            next_project, shapes(size), [project, project_got], after=(correlation,) if stage == 1 else ()
        )
        project_got = swap_row(message, [sum_order[stage]] * 2)
        summed = size
    (update,) = local(
        update_factor,
        [((rows, wide), BF)],
        [vectors, panel_factors, correlation, other_correlation],
        after=(message,),
    )

    for stage in range(1, row_stages):
        blocks, moved = local(
            lambda blocks, got, targets=n_row >> stage: split_targets(jnp.concatenate([blocks, got], 0), targets),
            halves,
            [blocks, blocks_got],
        )
        blocks_got = swap_row(moved, [move_order[stage]] * 2)
    move_places = [source_codes(move_order).index(code) for code in range(n_row)]
    (cyclic,) = local(
        lambda blocks, got: [pick_blocks(jnp.concatenate([blocks, got], 0), move_places)],
        [((rows, width), BF)],
        [blocks, blocks_got],
    )
    (project,) = local(
        lambda project, got: [(project + got.astype(F32)).astype(BF)],
        [((summed, width), BF)],
        [project, project_got],
        after=(cyclic, update),
    )
    (total,) = local(
        lambda update, cyclic, project: [
            cyclic.astype(F32) - jnp.dot(update[:, :summed], project, preferred_element_type=F32)
        ],
        [((rows, width), F32)],
        [update, cyclic, project],
    )
    for stage in reversed(range(row_stages - 1)):
        got = swap_row(project, [sum_order[stage]] * 2)
        project = got if row_stages == 2 else jnp.concatenate([project, got], 0)
    rest = project if row_stages == 2 else project[summed:]
    return finish(n_row, total, update, rest, summed)


def solution(mesh):
    return jax.shard_map(
        functools.partial(shards, mesh.shape["row"], mesh.shape["col"]),
        mesh=mesh,
        in_specs=(P("row", "col"), P("col"), P("col"), P(), P(), P(), P(None, "row", None), P()),
        out_specs=P("row", "col"),
        check_vma=False,
    )
```

```python
import functools

import jax
import jax.numpy as jnp
from jax import lax
from jax.experimental import pallas as pl
from jax.experimental.pallas import tpu as pltpu
from jax.sharding import PartitionSpec as P

BF = jnp.bfloat16
F32 = jnp.float32
HIGHEST = lax.Precision.HIGHEST
MIB = 2**20


def bit_orders(size, first):
    bits = list(range(first, size.bit_length() - 1))
    half = len(bits) // 2
    return bits, bits[half:] + bits[:half]


def target_codes(bits):
    if not bits:
        return [0]
    rest = target_codes(bits[1:])
    return rest + [(1 << bits[0]) | code for code in rest]


def source_codes(bits):
    codes = [0]
    for bit in bits:
        codes = codes + [(1 << bit) | code for code in codes]
    return codes


def is_even():
    return lax.rem(lax.axis_index("col"), 2) == 0


def select_code(even, pair):
    return pair[0] if pair[0] == pair[1] else jnp.where(even, pair[0], pair[1])


def row_bit(order, stage):
    return jnp.bitwise_and(lax.shift_right_logical(lax.axis_index("row"), order[stage]), 1) == 0


def swap_groups(value, axis, order):
    size = value.shape[axis]
    for stage in range(len(order) - 1):
        step = size >> (stage + 1)
        pieces = [lax.slice_in_dim(value, i, i + step, axis=axis) for i in range(0, size, step)]
        flipped = jnp.concatenate([pieces[i ^ 1] for i in range(len(pieces))], axis)
        value = jnp.where(row_bit(order, stage), value, flipped)
    return value


def local(fn, outs, values, after=()):
    outs = [jax.ShapeDtypeStruct(shape, dtype) for shape, dtype in outs]
    if any(v.shape[-1] % 128 or v.shape[-2] % 16 for v in list(values) + outs):
        return list(fn(*values))

    def kernel(*refs):
        ins = refs[:len(values)]
        results = fn(*[ref[...] for ref in ins])
        for ref, result in zip(refs[len(values) + len(after):], results):
            ref[...] = result

    return list(
        pl.pallas_call(
            kernel,
            in_specs=[pl.BlockSpec(memory_space=pltpu.VMEM)] * len(values)
            + [pl.BlockSpec(memory_space=pl.ANY)] * len(after),
            out_specs=[pl.BlockSpec(memory_space=pltpu.VMEM)] * len(outs),
            out_shape=[pltpu.VMEM(o.shape, o.dtype) for o in outs],
            compiler_params=pltpu.CompilerParams(vmem_limit_bytes=16 * MIB),
            cost_estimate=pl.CostEstimate(flops=1, bytes_accessed=1, transcendentals=0),
        )(*[pltpu.with_memory_space_constraint(v, pltpu.VMEM) for v in values], *after)
    )


def product_kernel(plan, width, chunks, depth, n_after, *refs):
    eig, pole_values, weights, roots, scale = refs[:5]
    outs = refs[5 + n_after:]
    poles = eig.shape[1]
    me = lax.axis_index("col")
    even = is_even()
    piece = width // chunks
    group = max(256 // piece, 1)
    pole_values = pole_values[...]
    weights = weights[...]
    for out, (chunk, codes) in zip(outs, plan):
        for place in range(0, len(codes), group):
            columns = [
                pl.ds(
                    pl.multiple_of(jnp.bitwise_xor(me, select_code(even, pair)) * width + chunk * piece, piece), piece
                )
                for pair in codes[place:place + group]
            ]
            near = jnp.concatenate([roots[:, at] for at in columns], 1)
            near = jnp.concatenate(
                [jnp.broadcast_to(near[:, j:j + 128], (128, 128)).T for j in range(0, near.shape[1], 128)], 0
            )
            total = None
            for k in range(0, poles, depth):
                gaps = pole_values[:, k:k + depth] - jnp.concatenate([near] * (depth // 128), 1)
                matrix = (weights[:, k:k + depth] / gaps).astype(BF)
                term = lax.dot_general(
                    eig[:, k:k + depth], matrix, (((1,), (1,)), ((), ())), preferred_element_type=F32
                )
                total = term if total is None else total + term
            total = total * jnp.concatenate([scale[:, at] for at in columns], 1)
            out[:, place * piece:place * piece + total.shape[1]] = total.astype(BF)


def plain_products(plan, row_codes, parts, chunks, operands):
    eigvecs, pole_order, pole_weight, root_gap, root_shift, column_weight = operands
    poles = eigvecs.shape[1]
    me = lax.axis_index("col")
    places = jnp.bitwise_xor(lax.axis_index("row"), jnp.array(row_codes, jnp.int32))
    ordered = eigvecs.reshape(len(row_codes), -1, poles)[places].reshape(eigvecs.shape)
    results = []
    for chunk, codes in plan:
        places = jnp.array([[a, b] for a, b in codes], jnp.int32)
        places = jnp.bitwise_xor(me, jnp.where(is_even(), places[:, 0], places[:, 1]))
        pick = lambda v: v.reshape(parts, chunks, -1)[places, chunk].reshape(-1)
        root_values = 2.0 * pick(root_gap).astype(F32) + 1.0 + pick(root_shift)
        numer = pole_weight[:, None] * pick(column_weight)[None, :]
        gaps = 2.0 * pole_order.astype(F32)[:, None] - root_values[None, :]
        results.append(jnp.dot(ordered, (numer / gaps).astype(BF), preferred_element_type=F32).astype(BF))
    return results


def products(plan, *, row_codes, parts, chunks, operands, state, after=()):
    rows, poles = operands[0].shape
    width = operands[3].shape[0] // parts
    if state is None:
        return plain_products(plan, row_codes, parts, chunks, operands)
    outs = [pltpu.VMEM((rows, width // chunks * len(codes)), BF) for _, codes in plan]
    return pl.pallas_call(
        functools.partial(product_kernel, plan, width, chunks, poles // 2, len(after)),
        in_specs=[pl.BlockSpec(memory_space=pltpu.VMEM)] * 5 + [pl.BlockSpec(memory_space=pl.ANY)] * len(after),
        out_specs=[pl.BlockSpec(memory_space=pltpu.VMEM)] * len(outs),
        out_shape=outs,
        compiler_params=pltpu.CompilerParams(vmem_limit_bytes=16 * MIB),
        cost_estimate=pl.CostEstimate(flops=1, bytes_accessed=1, transcendentals=0),
    )(*[pltpu.with_memory_space_constraint(operand, pltpu.VMEM) for operand in state], *after)


def panel_kernel(row_codes, row_orders, blocks, *refs):
    eig_hbm, panel_hbm, order_hbm, weight_hbm, gap_hbm, shift_hbm, scale_hbm = refs[:7]
    vectors_out, kept_out, message, correlation_out, eig, pole_values, weights, roots, scales = refs[7:16]
    panel, correlation, order, weight, gap, shift, scale, sem, eig_sem = refs[16:]
    even = is_even()
    row = lax.axis_index("row")
    block = panel.shape[1] // blocks
    targets = list(zip(*[target_codes(order) for order in row_orders]))
    at = lambda code: pl.ds(pl.multiple_of(jnp.bitwise_xor(row, code) * block, block), block)
    copies = [
        pltpu.make_async_copy(src, dst, sem.at[i])
        for i, (src, dst) in enumerate(
            [
                (panel_hbm, panel),
                (order_hbm, order),
                (weight_hbm, weight),
                (gap_hbm, gap),
                (shift_hbm, shift),
                (scale_hbm, scale),
            ]
        )
    ]
    for place, code in enumerate(row_codes):
        copies.append(
            pltpu.make_async_copy(
                eig_hbm.at[at(code)], eig.at[place * block:(place + 1) * block], eig_sem.at[place]
            )
        )
    for copy in copies:
        copy.start()
    for copy in copies[1:6]:
        copy.wait()
    pole_values[...] = (2.0 * order[...].astype(F32)).reshape(pole_values.shape)
    weights[...] = weight[...].reshape(weights.shape)
    roots[...] = (2.0 * gap[...].astype(F32) + 1.0 + shift[...]).reshape(roots.shape)
    scales[...] = scale[...].reshape(scales.shape)
    copies[0].wait()
    for code in range(blocks):
        vectors_out[0, code * block:(code + 1) * block] = panel[0, at(code)]
        vectors_out[1, code * block:(code + 1) * block] = panel[1, at(code)]
    core = jnp.where(even, 0, 1)
    correlation[...] = lax.dot_general(panel[1], panel[0], (((0,), (0,)), ((), ())), preferred_element_type=F32)
    near = correlation_out.shape[0]
    place = lax.shift_right_logical(lax.axis_index("col"), 1)
    part = correlation[pl.ds(pl.multiple_of(place * near, near), near)]
    correlation_out[...] = part
    message[:near] = part.astype(BF)
    for place, pair in enumerate(targets):
        value = panel[core, at(select_code(even, pair))]
        if place < blocks // 2:
            kept_out[place * block:(place + 1) * block] = value
        else:
            start = near + (place - blocks // 2) * block
            message[start:start + block] = value
    for copy in copies[6:]:
        copy.wait()


def panel_blocks(row_codes, row_orders, parts, panel_vectors, operands):
    panels, rows, width = panel_vectors.shape
    blocks = 1 << len(row_orders[0])
    near = width // parts
    poles, roots = operands[1].shape[0], operands[3].shape[0]
    eig_rows = operands[0].shape[0]
    outs = [
        pltpu.VMEM((panels, rows, width), BF),
        pltpu.VMEM((rows // 2, width), BF),
        pltpu.VMEM((near + rows // 2, width), BF),
        pltpu.VMEM((near, width), F32),
        pltpu.VMEM((eig_rows, poles), BF),
        pltpu.VMEM((1, poles), F32),
        pltpu.VMEM((1, poles), F32),
        pltpu.VMEM((1, roots), F32),
        pltpu.VMEM((1, roots), F32),
    ]
    results = pl.pallas_call(
        functools.partial(panel_kernel, row_codes, row_orders, blocks),
        in_specs=[pl.BlockSpec(memory_space=pl.ANY)] * 7,
        out_specs=[pl.BlockSpec(memory_space=pltpu.VMEM)] * len(outs),
        out_shape=outs,
        scratch_shapes=[
            pltpu.VMEM((panels, rows, width), BF),
            pltpu.VMEM((width, width), F32),
            pltpu.VMEM((poles,), jnp.int32),
            pltpu.VMEM((poles,), F32),
            pltpu.VMEM((roots,), jnp.int32),
            pltpu.VMEM((roots,), F32),
            pltpu.VMEM((roots,), F32),
            pltpu.SemaphoreType.DMA((6,)),
            pltpu.SemaphoreType.DMA((blocks,)),
        ],
        compiler_params=pltpu.CompilerParams(vmem_limit_bytes=16 * MIB),
        cost_estimate=pl.CostEstimate(flops=1, bytes_accessed=1, transcendentals=0),
    )(*[pltpu.with_memory_space_constraint(v, pltpu.HBM) for v in (operands[0], panel_vectors, *operands[1:])])
    return results[:4], results[4:]


def finish_kernel(blocks, start, total, update, project, out_hbm, result, sem):
    block = total.shape[0] // blocks
    row = lax.axis_index("row")
    value = total[...] - jnp.dot(update[:, start:], project[...], preferred_element_type=F32)
    result[...] = value.astype(BF)
    copies = []
    for code in range(blocks):
        at = pl.multiple_of(jnp.bitwise_xor(row, code) * block, block)
        copies.append(
            pltpu.make_async_copy(
                result.at[code * block:(code + 1) * block], out_hbm.at[pl.ds(at, block)], sem.at[code]
            )
        )
        copies[-1].start()
    for copy in copies:
        copy.wait()


def finish(blocks, total, update, project, start):
    rows, width = total.shape
    if width % 128:
        result = (total - jnp.dot(update[:, start:], project, preferred_element_type=F32)).astype(BF)
        places = jnp.bitwise_xor(lax.axis_index("row"), jnp.arange(blocks))
        return result.reshape(blocks, -1, width)[places].reshape(rows, width)
    return pl.pallas_call(
        functools.partial(finish_kernel, blocks, start),
        in_specs=[pl.BlockSpec(memory_space=pltpu.VMEM)] * 3,
        out_specs=pl.BlockSpec(memory_space=pl.ANY),
        out_shape=jax.ShapeDtypeStruct((rows, width), BF),
        scratch_shapes=[pltpu.VMEM((rows, width), BF), pltpu.SemaphoreType.DMA((blocks,))],
        compiler_params=pltpu.CompilerParams(vmem_limit_bytes=16 * MIB),
        cost_estimate=pl.CostEstimate(flops=1, bytes_accessed=1, transcendentals=0),
    )(*[pltpu.with_memory_space_constraint(v, pltpu.VMEM) for v in (total, update, project)])


def split_dot(left, right):
    def parts(value):
        if value.dtype == BF:
            return [value]
        high = value.astype(BF)
        return [high, (value - high.astype(F32)).astype(BF)]

    total = None
    for i, a in enumerate(parts(left)):
        for j, b in enumerate(parts(right)):
            if i + j < 2:
                term = jnp.dot(a, b, preferred_element_type=F32)
                total = term if total is None else total + term
    return total


def shards(
    n_row,
    n_col,
    eigvecs,
    pole_order,
    pole_weight,
    root_gap,
    root_shift,
    column_weight,
    panel_vectors,
    panel_factors,
):
    col_orders = bit_orders(n_col, 1)
    row_orders = bit_orders(n_row, 0)
    col_stages = len(col_orders[0])
    row_stages = len(row_orders[0])
    rows = eigvecs.shape[0]
    block = rows // n_row
    panel_width = panel_vectors.shape[2]
    parts = n_col // 2
    near = panel_width // parts
    width = root_gap.shape[0] // n_col
    chunks = 2 if width % 256 == 0 else 1
    piece = width // chunks
    sum_order = row_orders[0]
    move_order = sum_order[::-1]

    def swap_cores(value):
        return lax.ppermute(value, "col", [(i, i ^ 1) for i in range(n_col)])

    def swap_col(value, stage):
        return lax.ppermute(value, "col", [(i, i ^ (1 << col_orders[i % 2][stage])) for i in range(n_col)])

    def swap_row(value, bits):
        pairs = [(r * n_col + c, (r ^ (1 << bits[c % 2])) * n_col + c) for r in range(n_row) for c in range(n_col)]
        return lax.ppermute(value, ("row", "col"), pairs)

    def split_targets(value, targets):
        step = targets * block
        kept = [value[i:i + step // 2] for i in range(0, value.shape[0], step)]
        sent = [value[i + step // 2:i + step] for i in range(0, value.shape[0], step)]
        return jnp.concatenate(kept, 0), jnp.concatenate(sent, 0)

    def pick_blocks(value, places):
        return jnp.concatenate([value[i * block:(i + 1) * block] for i in places], 0)

    targets = target_codes(move_order)
    own_codes = list(zip(*[target_codes(order) for order in col_orders]))
    other_codes = [(1 ^ odd, 1 ^ even) for even, odd in own_codes]
    half = len(own_codes) // 2
    operands = (eigvecs, pole_order, pole_weight, root_gap, root_shift, column_weight)
    (vectors, kept, message, correlation), state = panel_blocks(
        targets, row_orders, parts, panel_vectors, operands
    )
    if width % (128 * chunks) or eigvecs.shape[1] % 256:
        state = None
    multiply = functools.partial(
        products, row_codes=targets, parts=n_col, chunks=chunks, operands=operands, state=state
    )
    got_sent, own_sent, made = [], [], ()
    for chunk in range(chunks):
        other, own = multiply([(chunk, other_codes[half:]), (chunk, own_codes[half:])], after=made)
        got_sent.append(swap_cores(other))
        own_sent.append(own)
        made = (own,)
    long = half * piece
    sent = []
    for own, got in zip(own_sent, got_sent):
        (value,) = local(
            lambda own, got: [(own.astype(F32) + got.astype(F32)).astype(BF)],
            [((rows, long), BF)],
            [own, got],
            after=(*made, *sent),
        )
        sent.append(value)
    got = [swap_col(message, 0) for message in sent]
    other_kept = multiply([(chunk, other_codes[:half]) for chunk in range(chunks)], after=(sent[-1],))
    got_kept = [swap_cores(value) for value in other_kept]
    own_kept = multiply([(chunk, own_codes[:half]) for chunk in range(chunks)], after=(other_kept[0],))

    current = [[own, other, new] for own, other, new in zip(own_kept, got_kept, got)]
    for stage in range(1, col_stages):
        long //= 2

        def next_sums(*values, long=long):
            count = len(values) // chunks
            totals = [sum(v.astype(F32) for v in values[i:i + count]) for i in range(0, len(values), count)]
            out = jnp.concatenate([total[:, long:] for total in totals], 1).astype(BF)
            return *[total[:, :long] for total in totals], out

        *totals, col_message = local(
            next_sums,
            [((rows, long), F32)] * chunks + [((rows, chunks * long), BF)],
            sum(current, []),
        )
        if stage == 1:
            first_message = col_message
        got = swap_col(col_message, stage)
        current = [[total, got] for total in totals]
        if stage < col_stages - 1:
            current = [[total, got[:, i * long:(i + 1) * long]] for i, total in enumerate(totals)]

    for stage in range(row_stages):
        panel_got = swap_row(message, [order[stage] for order in row_orders])

        if stage < row_stages - 1:

            def next_panel(kept, correlation, got, targets=n_row >> (stage + 1)):
                correlation = correlation + got[:near].astype(F32)
                kept, moved = split_targets(jnp.concatenate([kept, got[near:]], 0), targets)
                return kept, jnp.concatenate([correlation.astype(BF), moved], 0), correlation

            kept, message, correlation = local(
                next_panel,
                [((rows // 2, panel_width), BF), ((near + rows // 2, panel_width), BF), ((near, panel_width), F32)],
                [kept, correlation, panel_got],
                after=(other_kept[0],),
            )
    panel_places = [[source_codes(order).index(code) for code in range(n_row)] for order in row_orders]

    first_rows = 3 * rows // 4

    def panel_done(kept, correlation, got):
        correlation = (correlation + got[:near].astype(F32)).astype(BF)
        value = jnp.concatenate([kept, got[near:]], 0)
        orders = [pick_blocks(value, places).astype(F32) for places in panel_places]
        value = jnp.where(is_even(), orders[0], orders[1]).astype(BF)
        return value, correlation, value[:first_rows], value[first_rows:]

    mine, correlation, *mine_sent = local(
        panel_done,
        [((r, panel_width), BF) for r in (rows, near, first_rows, rows - first_rows)],
        [kept, correlation, panel_got],
        after=(first_message,),
    )
    other = [swap_cores(value) for value in mine_sent]

    wide = 2 * panel_width
    summed = wide // 2 if row_stages > 1 else wide

    def projections(mine, *values):
        other, values = values[:2], values[2:]
        merged = jnp.concatenate(values[:chunks], 1) + jnp.concatenate(values[chunks:], 1).astype(F32)
        merged = merged.astype(BF)
        dims = (((0,), (0,)), ((), ()))
        project = jnp.concatenate(
            [
                lax.dot_general(pick_blocks(v, targets), merged, dims, preferred_element_type=F32)
                for v in (mine, jnp.concatenate(other, 0))
            ],
            0,
        )
        project = swap_groups(project, 0, sum_order)
        out = project if row_stages == 1 else project[summed:]
        return project[:summed], out.astype(BF), *split_targets(merged, n_row)

    shapes = lambda size: [((size, width), F32), ((size, width), BF)]
    halves = [((rows // 2, width), BF)] * 2
    last_got = [current[0][1]] if col_stages > 1 else [c[1] for c in current]
    project, message, blocks, moved = local(
        projections,
        shapes(summed) + halves,
        [mine, *other, *[c[0] for c in current], *last_got],
    )
    project_got = swap_row(message, [sum_order[0]] * 2)
    blocks_got = swap_row(moved, [move_order[0]] * 2)

    def join(mine, got, stage):
        shift = select_code(is_even(), (col_orders[0][stage], col_orders[1][stage]))
        low = jnp.bitwise_and(lax.shift_right_logical(lax.axis_index("col"), shift), 1) == 0
        mine, got = mine.astype(F32), got.astype(F32)
        return jnp.concatenate([jnp.where(low, mine, got), jnp.where(low, got, mine)], 0)

    joined = near
    for stage in range(col_stages - 1):
        joined *= 2
        (correlation,) = local(
            lambda mine, got, stage=stage: [join(mine, got, stage).astype(BF)],
            [((joined, panel_width), BF)],
            [correlation, swap_col(correlation, stage)],
            after=(message,),
        )
    other_correlation = swap_col(correlation, col_stages - 1)
    part_orders = [source_codes([bit - 1 for bit in order]) for order in col_orders]
    part_orders = [[order.index(part) for part in range(parts)] for order in part_orders]

    def update_factor(vectors, factors, mine, other):
        even = is_even()
        correlation = join(mine, other, col_stages - 1)
        ordered = [
            jnp.concatenate([correlation[i * near:(i + 1) * near] for i in order], 0) for order in part_orders
        ]
        correlation = jnp.where(even, ordered[0], ordered[1]).astype(BF)
        across = split_dot(vectors[1], split_dot(factors[1], correlation))
        first = split_dot(vectors[0].astype(F32) - across, factors[0])
        second = split_dot(vectors[1], factors[1])
        update = jnp.concatenate([jnp.where(even, first, second), jnp.where(even, second, first)], 1)
        return [swap_groups(update, 1, sum_order).astype(BF)]

    for stage in range(1, row_stages):
        last = stage == row_stages - 1
        size = summed if last else summed // 2

        def next_project(project, got, last=last, size=size):
            total = project + got.astype(F32)
            return total[:size], (total if last else total[size:]).astype(BF)

        project, message = local(
            next_project, shapes(size), [project, project_got], after=(correlation,) if stage == 1 else ()
        )
        project_got = swap_row(message, [sum_order[stage]] * 2)
        summed = size
    (update,) = local(
        update_factor,
        [((rows, wide), BF)],
        [vectors, panel_factors, correlation, other_correlation],
        after=(message,),
    )

    for stage in range(1, row_stages):
        blocks, moved = local(
            lambda blocks, got, targets=n_row >> stage: split_targets(jnp.concatenate([blocks, got], 0), targets),
            halves,
            [blocks, blocks_got],
        )
        blocks_got = swap_row(moved, [move_order[stage]] * 2)
    move_places = [source_codes(move_order).index(code) for code in range(n_row)]
    (cyclic,) = local(
        lambda blocks, got: [pick_blocks(jnp.concatenate([blocks, got], 0), move_places)],
        [((rows, width), BF)],
        [blocks, blocks_got],
    )
    (project,) = local(
        lambda project, got: [(project + got.astype(F32)).astype(BF)],
        [((summed, width), BF)],
        [project, project_got],
        after=(cyclic, update),
    )
    (total,) = local(
        lambda update, cyclic, project: [
            cyclic.astype(F32) - jnp.dot(update[:, :summed], project, preferred_element_type=F32)
        ],
        [((rows, width), F32)],
        [update, cyclic, project],
    )
    for stage in reversed(range(row_stages - 1)):
        got = swap_row(project, [sum_order[stage]] * 2)
        project = got if row_stages == 2 else jnp.concatenate([project, got], 0)
    rest = project if row_stages == 2 else project[summed:]
    return finish(n_row, total, update, rest, summed)


def solution(mesh):
    return jax.shard_map(
        functools.partial(shards, mesh.shape["row"], mesh.shape["col"]),
        mesh=mesh,
        in_specs=(P("row", "col"), P("col"), P("col"), P(), P(), P(), P(None, "row", None), P()),
        out_specs=P("row", "col"),
        check_vma=False,
    )
```

```python
import functools

import jax
import jax.numpy as jnp
from jax import lax
from jax.experimental import pallas as pl
from jax.experimental.pallas import tpu as pltpu
from jax.sharding import PartitionSpec as P

BF = jnp.bfloat16
F32 = jnp.float32
HIGHEST = lax.Precision.HIGHEST
MIB = 2**20


def bit_orders(size, first):
    bits = list(range(first, size.bit_length() - 1))
    half = len(bits) // 2
    return bits, bits[half:] + bits[:half]


def target_codes(bits):
    if not bits:
        return [0]
    rest = target_codes(bits[1:])
    return rest + [(1 << bits[0]) | code for code in rest]


def source_codes(bits):
    codes = [0]
    for bit in bits:
        codes = codes + [(1 << bit) | code for code in codes]
    return codes


def is_even():
    return lax.rem(lax.axis_index("col"), 2) == 0


def select_code(even, pair):
    return pair[0] if pair[0] == pair[1] else jnp.where(even, pair[0], pair[1])


def row_bit(order, stage):
    return jnp.bitwise_and(lax.shift_right_logical(lax.axis_index("row"), order[stage]), 1) == 0


def swap_groups(value, axis, order):
    size = value.shape[axis]
    for stage in range(len(order) - 1):
        step = size >> (stage + 1)
        pieces = [lax.slice_in_dim(value, i, i + step, axis=axis) for i in range(0, size, step)]
        flipped = jnp.concatenate([pieces[i ^ 1] for i in range(len(pieces))], axis)
        value = jnp.where(row_bit(order, stage), value, flipped)
    return value


def local(fn, outs, values, after=(), cost=1):
    outs = [jax.ShapeDtypeStruct(shape, dtype) for shape, dtype in outs]
    if any(v.shape[-1] % 128 or v.shape[-2] % 16 for v in list(values) + outs):
        return list(fn(*values))

    def kernel(*refs):
        ins = refs[:len(values)]
        results = fn(*[ref[...] for ref in ins])
        for ref, result in zip(refs[len(values) + len(after):], results):
            ref[...] = result

    return list(
        pl.pallas_call(
            kernel,
            in_specs=[pl.BlockSpec(memory_space=pltpu.VMEM)] * len(values)
            + [pl.BlockSpec(memory_space=pl.ANY)] * len(after),
            out_specs=[pl.BlockSpec(memory_space=pltpu.VMEM)] * len(outs),
            out_shape=[pltpu.VMEM(o.shape, o.dtype) for o in outs],
            compiler_params=pltpu.CompilerParams(vmem_limit_bytes=16 * MIB),
            cost_estimate=pl.CostEstimate(flops=cost, bytes_accessed=1, transcendentals=0),
        )(*[pltpu.with_memory_space_constraint(v, pltpu.VMEM) for v in values], *after)
    )


def product_kernel(plan, width, chunks, depth, n_after, *refs):
    eig, pole_values, weights, roots, scale = refs[:5]
    outs = refs[5 + n_after:]
    poles = eig.shape[1]
    me = lax.axis_index("col")
    even = is_even()
    piece = width // chunks
    group = max(256 // piece, 1)
    pole_values = pole_values[...]
    weights = weights[...]
    for out, (chunk, codes) in zip(outs, plan):
        for place in range(0, len(codes), group):
            columns = [
                pl.ds(
                    pl.multiple_of(jnp.bitwise_xor(me, select_code(even, pair)) * width + chunk * piece, piece), piece
                )
                for pair in codes[place:place + group]
            ]
            near = jnp.concatenate([roots[:, at] for at in columns], 1)
            near = jnp.concatenate(
                [jnp.broadcast_to(near[:, j:j + 128], (128, 128)).T for j in range(0, near.shape[1], 128)], 0
            )
            total = None
            for k in range(0, poles, depth):
                gaps = pole_values[:, k:k + depth] - jnp.concatenate([near] * (depth // 128), 1)
                matrix = (weights[:, k:k + depth] / gaps).astype(BF)
                term = lax.dot_general(
                    eig[:, k:k + depth], matrix, (((1,), (1,)), ((), ())), preferred_element_type=F32
                )
                total = term if total is None else total + term
            total = total * jnp.concatenate([scale[:, at] for at in columns], 1)
            out[:, place * piece:place * piece + total.shape[1]] = total.astype(BF)


def plain_products(plan, row_codes, parts, chunks, operands):
    eigvecs, pole_order, pole_weight, root_gap, root_shift, column_weight = operands
    poles = eigvecs.shape[1]
    me = lax.axis_index("col")
    places = jnp.bitwise_xor(lax.axis_index("row"), jnp.array(row_codes, jnp.int32))
    ordered = eigvecs.reshape(len(row_codes), -1, poles)[places].reshape(eigvecs.shape)
    results = []
    for chunk, codes in plan:
        places = jnp.array([[a, b] for a, b in codes], jnp.int32)
        places = jnp.bitwise_xor(me, jnp.where(is_even(), places[:, 0], places[:, 1]))
        pick = lambda v: v.reshape(parts, chunks, -1)[places, chunk].reshape(-1)
        root_values = 2.0 * pick(root_gap).astype(F32) + 1.0 + pick(root_shift)
        numer = pole_weight[:, None] * pick(column_weight)[None, :]
        gaps = 2.0 * pole_order.astype(F32)[:, None] - root_values[None, :]
        results.append(jnp.dot(ordered, (numer / gaps).astype(BF), preferred_element_type=F32).astype(BF))
    return results


def products(plan, *, row_codes, parts, chunks, operands, state, after=()):
    rows, poles = operands[0].shape
    width = operands[3].shape[0] // parts
    if state is None:
        return plain_products(plan, row_codes, parts, chunks, operands)
    outs = [pltpu.VMEM((rows, width // chunks * len(codes)), BF) for _, codes in plan]
    return pl.pallas_call(
        functools.partial(product_kernel, plan, width, chunks, poles // 2, len(after)),
        in_specs=[pl.BlockSpec(memory_space=pltpu.VMEM)] * 5 + [pl.BlockSpec(memory_space=pl.ANY)] * len(after),
        out_specs=[pl.BlockSpec(memory_space=pltpu.VMEM)] * len(outs),
        out_shape=outs,
        compiler_params=pltpu.CompilerParams(vmem_limit_bytes=16 * MIB),
        cost_estimate=pl.CostEstimate(flops=1, bytes_accessed=1, transcendentals=0),
    )(*[pltpu.with_memory_space_constraint(operand, pltpu.VMEM) for operand in state], *after)


def panel_kernel(row_codes, row_orders, blocks, *refs):
    eig_hbm, panel_hbm, order_hbm, weight_hbm, gap_hbm, shift_hbm, scale_hbm = refs[:7]
    vectors_out, kept_out, message, correlation_out, eig, pole_values, weights, roots, scales = refs[7:16]
    panel, correlation, order, weight, gap, shift, scale, sem, eig_sem = refs[16:]
    even = is_even()
    row = lax.axis_index("row")
    block = panel.shape[1] // blocks
    targets = list(zip(*[target_codes(order) for order in row_orders]))
    at = lambda code: pl.ds(pl.multiple_of(jnp.bitwise_xor(row, code) * block, block), block)
    copies = [
        pltpu.make_async_copy(src, dst, sem.at[i])
        for i, (src, dst) in enumerate(
            [
                (panel_hbm, panel),
                (order_hbm, order),
                (weight_hbm, weight),
                (gap_hbm, gap),
                (shift_hbm, shift),
                (scale_hbm, scale),
            ]
        )
    ]
    for place, code in enumerate(row_codes):
        copies.append(
            pltpu.make_async_copy(
                eig_hbm.at[at(code)], eig.at[place * block:(place + 1) * block], eig_sem.at[place]
            )
        )
    for copy in copies:
        copy.start()
    for copy in copies[1:6]:
        copy.wait()
    pole_values[...] = (2.0 * order[...].astype(F32)).reshape(pole_values.shape)
    weights[...] = weight[...].reshape(weights.shape)
    roots[...] = (2.0 * gap[...].astype(F32) + 1.0 + shift[...]).reshape(roots.shape)
    scales[...] = scale[...].reshape(scales.shape)
    copies[0].wait()
    for code in range(blocks):
        vectors_out[0, code * block:(code + 1) * block] = panel[0, at(code)]
        vectors_out[1, code * block:(code + 1) * block] = panel[1, at(code)]
    core = jnp.where(even, 0, 1)
    correlation[...] = lax.dot_general(panel[1], panel[0], (((0,), (0,)), ((), ())), preferred_element_type=F32)
    near = correlation_out.shape[0]
    place = lax.shift_right_logical(lax.axis_index("col"), 1)
    part = correlation[pl.ds(pl.multiple_of(place * near, near), near)]
    correlation_out[...] = part
    message[:near] = part.astype(BF)
    for place, pair in enumerate(targets):
        value = panel[core, at(select_code(even, pair))]
        if place < blocks // 2:
            kept_out[place * block:(place + 1) * block] = value
        else:
            start = near + (place - blocks // 2) * block
            message[start:start + block] = value
    for copy in copies[6:]:
        copy.wait()


def panel_blocks(row_codes, row_orders, parts, panel_vectors, operands):
    panels, rows, width = panel_vectors.shape
    blocks = 1 << len(row_orders[0])
    near = width // parts
    poles, roots = operands[1].shape[0], operands[3].shape[0]
    eig_rows = operands[0].shape[0]
    outs = [
        pltpu.VMEM((panels, rows, width), BF),
        pltpu.VMEM((rows // 2, width), BF),
        pltpu.VMEM((near + rows // 2, width), BF),
        pltpu.VMEM((near, width), F32),
        pltpu.VMEM((eig_rows, poles), BF),
        pltpu.VMEM((1, poles), F32),
        pltpu.VMEM((1, poles), F32),
        pltpu.VMEM((1, roots), F32),
        pltpu.VMEM((1, roots), F32),
    ]
    results = pl.pallas_call(
        functools.partial(panel_kernel, row_codes, row_orders, blocks),
        in_specs=[pl.BlockSpec(memory_space=pl.ANY)] * 7,
        out_specs=[pl.BlockSpec(memory_space=pltpu.VMEM)] * len(outs),
        out_shape=outs,
        scratch_shapes=[
            pltpu.VMEM((panels, rows, width), BF),
            pltpu.VMEM((width, width), F32),
            pltpu.VMEM((poles,), jnp.int32),
            pltpu.VMEM((poles,), F32),
            pltpu.VMEM((roots,), jnp.int32),
            pltpu.VMEM((roots,), F32),
            pltpu.VMEM((roots,), F32),
            pltpu.SemaphoreType.DMA((6,)),
            pltpu.SemaphoreType.DMA((blocks,)),
        ],
        compiler_params=pltpu.CompilerParams(vmem_limit_bytes=16 * MIB),
        cost_estimate=pl.CostEstimate(flops=1, bytes_accessed=1, transcendentals=0),
    )(*[pltpu.with_memory_space_constraint(v, pltpu.HBM) for v in (operands[0], panel_vectors, *operands[1:])])
    return results[:4], results[4:]


def finish_kernel(blocks, start, total, update, project, out_hbm, result, sem):
    block = total.shape[0] // blocks
    row = lax.axis_index("row")
    value = total[...] - jnp.dot(update[:, start:], project[...], preferred_element_type=F32)
    result[...] = value.astype(BF)
    copies = []
    for code in range(blocks):
        at = pl.multiple_of(jnp.bitwise_xor(row, code) * block, block)
        copies.append(
            pltpu.make_async_copy(
                result.at[code * block:(code + 1) * block], out_hbm.at[pl.ds(at, block)], sem.at[code]
            )
        )
        copies[-1].start()
    for copy in copies:
        copy.wait()


def finish(blocks, total, update, project, start):
    rows, width = total.shape
    if width % 128:
        result = (total - jnp.dot(update[:, start:], project, preferred_element_type=F32)).astype(BF)
        places = jnp.bitwise_xor(lax.axis_index("row"), jnp.arange(blocks))
        return result.reshape(blocks, -1, width)[places].reshape(rows, width)
    return pl.pallas_call(
        functools.partial(finish_kernel, blocks, start),
        in_specs=[pl.BlockSpec(memory_space=pltpu.VMEM)] * 3,
        out_specs=pl.BlockSpec(memory_space=pl.ANY),
        out_shape=jax.ShapeDtypeStruct((rows, width), BF),
        scratch_shapes=[pltpu.VMEM((rows, width), BF), pltpu.SemaphoreType.DMA((blocks,))],
        compiler_params=pltpu.CompilerParams(vmem_limit_bytes=16 * MIB),
        cost_estimate=pl.CostEstimate(flops=1, bytes_accessed=1, transcendentals=0),
    )(*[pltpu.with_memory_space_constraint(v, pltpu.VMEM) for v in (total, update, project)])


def split_dot(left, right):
    def parts(value):
        if value.dtype == BF:
            return [value]
        high = value.astype(BF)
        return [high, (value - high.astype(F32)).astype(BF)]

    total = None
    for i, a in enumerate(parts(left)):
        for j, b in enumerate(parts(right)):
            if i + j < 2:
                term = jnp.dot(a, b, preferred_element_type=F32)
                total = term if total is None else total + term
    return total


def shards(
    n_row,
    n_col,
    eigvecs,
    pole_order,
    pole_weight,
    root_gap,
    root_shift,
    column_weight,
    panel_vectors,
    panel_factors,
):
    col_orders = bit_orders(n_col, 1)
    row_orders = bit_orders(n_row, 0)
    col_stages = len(col_orders[0])
    row_stages = len(row_orders[0])
    rows = eigvecs.shape[0]
    block = rows // n_row
    panel_width = panel_vectors.shape[2]
    parts = n_col // 2
    near = panel_width // parts
    width = root_gap.shape[0] // n_col
    chunks = 2 if width % 256 == 0 else 1
    piece = width // chunks
    sum_order = row_orders[0]
    move_order = sum_order[::-1]

    def swap_cores(value):
        return lax.ppermute(value, "col", [(i, i ^ 1) for i in range(n_col)])

    def swap_col(value, stage):
        return lax.ppermute(value, "col", [(i, i ^ (1 << col_orders[i % 2][stage])) for i in range(n_col)])

    def swap_row(value, bits):
        pairs = [(r * n_col + c, (r ^ (1 << bits[c % 2])) * n_col + c) for r in range(n_row) for c in range(n_col)]
        return lax.ppermute(value, ("row", "col"), pairs)

    def split_targets(value, targets):
        step = targets * block
        kept = [value[i:i + step // 2] for i in range(0, value.shape[0], step)]
        sent = [value[i + step // 2:i + step] for i in range(0, value.shape[0], step)]
        return jnp.concatenate(kept, 0), jnp.concatenate(sent, 0)

    def pick_blocks(value, places):
        return jnp.concatenate([value[i * block:(i + 1) * block] for i in places], 0)

    targets = target_codes(move_order)
    own_codes = list(zip(*[target_codes(order) for order in col_orders]))
    other_codes = [(1 ^ odd, 1 ^ even) for even, odd in own_codes]
    half = len(own_codes) // 2
    operands = (eigvecs, pole_order, pole_weight, root_gap, root_shift, column_weight)
    (vectors, kept, message, correlation), state = panel_blocks(
        targets, row_orders, parts, panel_vectors, operands
    )
    if width % (128 * chunks) or eigvecs.shape[1] % 256:
        state = None
    multiply = functools.partial(
        products, row_codes=targets, parts=n_col, chunks=chunks, operands=operands, state=state
    )
    got_sent, own_sent, made = [], [], ()
    for chunk in range(chunks):
        other, own = multiply([(chunk, other_codes[half:]), (chunk, own_codes[half:])], after=made)
        got_sent.append(swap_cores(other))
        own_sent.append(own)
        made = (own,)
    long = half * piece
    sent = []
    for own, got in zip(own_sent, got_sent):
        (value,) = local(
            lambda own, got: [(own.astype(F32) + got.astype(F32)).astype(BF)],
            [((rows, long), BF)],
            [own, got],
            after=(*made, *sent),
        )
        sent.append(value)
    got = [swap_col(message, 0) for message in sent]
    other_kept = multiply([(chunk, other_codes[:half]) for chunk in range(chunks)], after=(sent[-1],))
    got_kept = [swap_cores(value) for value in other_kept]
    own_kept = multiply([(chunk, own_codes[:half]) for chunk in range(chunks)], after=(other_kept[0],))

    current = [[own, other, new] for own, other, new in zip(own_kept, got_kept, got)]
    for stage in range(1, col_stages):
        long //= 2

        def next_sums(*values, long=long):
            count = len(values) // chunks
            totals = [sum(v.astype(F32) for v in values[i:i + count]) for i in range(0, len(values), count)]
            out = jnp.concatenate([total[:, long:] for total in totals], 1).astype(BF)
            return *[total[:, :long] for total in totals], out

        *totals, col_message = local(
            next_sums,
            [((rows, long), F32)] * chunks + [((rows, chunks * long), BF)],
            sum(current, []),
        )
        if stage == 1:
            first_message = col_message
        got = swap_col(col_message, stage)
        current = [[total, got] for total in totals]
        if stage < col_stages - 1:
            current = [[total, got[:, i * long:(i + 1) * long]] for i, total in enumerate(totals)]

    for stage in range(row_stages):
        panel_got = swap_row(message, [order[stage] for order in row_orders])

        if stage < row_stages - 1:

            def next_panel(kept, correlation, got, targets=n_row >> (stage + 1)):
                correlation = correlation + got[:near].astype(F32)
                kept, moved = split_targets(jnp.concatenate([kept, got[near:]], 0), targets)
                return kept, jnp.concatenate([correlation.astype(BF), moved], 0), correlation

            kept, message, correlation = local(
                next_panel,
                [((rows // 2, panel_width), BF), ((near + rows // 2, panel_width), BF), ((near, panel_width), F32)],
                [kept, correlation, panel_got],
                after=(sent[-1],),
                cost=5000000000,
            )
    panel_places = [[source_codes(order).index(code) for code in range(n_row)] for order in row_orders]

    first_rows = 3 * rows // 4

    def panel_done(kept, correlation, got):
        correlation = (correlation + got[:near].astype(F32)).astype(BF)
        value = jnp.concatenate([kept, got[near:]], 0)
        orders = [pick_blocks(value, places).astype(F32) for places in panel_places]
        value = jnp.where(is_even(), orders[0], orders[1]).astype(BF)
        return value, correlation, value[:first_rows], value[first_rows:]

    mine, correlation, *mine_sent = local(
        panel_done,
        [((r, panel_width), BF) for r in (rows, near, first_rows, rows - first_rows)],
        [kept, correlation, panel_got],
        after=(first_message,),
    )
    other = [swap_cores(value) for value in mine_sent]

    wide = 2 * panel_width
    summed = wide // 2 if row_stages > 1 else wide

    def projections(mine, *values):
        other, values = values[:2], values[2:]
        merged = jnp.concatenate(values[:chunks], 1) + jnp.concatenate(values[chunks:], 1).astype(F32)
        merged = merged.astype(BF)
        dims = (((0,), (0,)), ((), ()))
        project = jnp.concatenate(
            [
                lax.dot_general(pick_blocks(v, targets), merged, dims, preferred_element_type=F32)
                for v in (mine, jnp.concatenate(other, 0))
            ],
            0,
        )
        project = swap_groups(project, 0, sum_order)
        out = project if row_stages == 1 else project[summed:]
        return project[:summed], out.astype(BF), *split_targets(merged, n_row)

    shapes = lambda size: [((size, width), F32), ((size, width), BF)]
    halves = [((rows // 2, width), BF)] * 2
    last_got = [current[0][1]] if col_stages > 1 else [c[1] for c in current]
    project, message, blocks, moved = local(
        projections,
        shapes(summed) + halves,
        [mine, *other, *[c[0] for c in current], *last_got],
    )
    project_got = swap_row(message, [sum_order[0]] * 2)
    blocks_got = swap_row(moved, [move_order[0]] * 2)

    def join(mine, got, stage):
        shift = select_code(is_even(), (col_orders[0][stage], col_orders[1][stage]))
        low = jnp.bitwise_and(lax.shift_right_logical(lax.axis_index("col"), shift), 1) == 0
        mine, got = mine.astype(F32), got.astype(F32)
        return jnp.concatenate([jnp.where(low, mine, got), jnp.where(low, got, mine)], 0)

    joined = near
    for stage in range(col_stages - 1):
        joined *= 2
        (correlation,) = local(
            lambda mine, got, stage=stage: [join(mine, got, stage).astype(BF)],
            [((joined, panel_width), BF)],
            [correlation, swap_col(correlation, stage)],
            after=(message,),
        )
    other_correlation = swap_col(correlation, col_stages - 1)
    part_orders = [source_codes([bit - 1 for bit in order]) for order in col_orders]
    part_orders = [[order.index(part) for part in range(parts)] for order in part_orders]

    def update_factor(vectors, factors, mine, other):
        even = is_even()
        correlation = join(mine, other, col_stages - 1)
        ordered = [
            jnp.concatenate([correlation[i * near:(i + 1) * near] for i in order], 0) for order in part_orders
        ]
        correlation = jnp.where(even, ordered[0], ordered[1]).astype(BF)
        across = split_dot(vectors[1], split_dot(factors[1], correlation))
        first = split_dot(vectors[0].astype(F32) - across, factors[0])
        second = split_dot(vectors[1], factors[1])
        update = jnp.concatenate([jnp.where(even, first, second), jnp.where(even, second, first)], 1)
        return [swap_groups(update, 1, sum_order).astype(BF)]

    for stage in range(1, row_stages):
        last = stage == row_stages - 1
        size = summed if last else summed // 2

        def next_project(project, got, last=last, size=size):
            total = project + got.astype(F32)
            return total[:size], (total if last else total[size:]).astype(BF)

        project, message = local(
            next_project, shapes(size), [project, project_got], after=(correlation,) if stage == 1 else ()
        )
        project_got = swap_row(message, [sum_order[stage]] * 2)
        summed = size
    (update,) = local(
        update_factor,
        [((rows, wide), BF)],
        [vectors, panel_factors, correlation, other_correlation],
        after=(message,),
        cost=1000000000,
    )

    for stage in range(1, row_stages):
        blocks, moved = local(
            lambda blocks, got, targets=n_row >> stage: split_targets(jnp.concatenate([blocks, got], 0), targets),
            halves,
            [blocks, blocks_got],
        )
        blocks_got = swap_row(moved, [move_order[stage]] * 2)
    move_places = [source_codes(move_order).index(code) for code in range(n_row)]
    (cyclic,) = local(
        lambda blocks, got: [pick_blocks(jnp.concatenate([blocks, got], 0), move_places)],
        [((rows, width), BF)],
        [blocks, blocks_got],
    )
    (project,) = local(
        lambda project, got: [(project + got.astype(F32)).astype(BF)],
        [((summed, width), BF)],
        [project, project_got],
    )
    (total,) = local(
        lambda update, cyclic, project: [
            cyclic.astype(F32) - jnp.dot(update[:, :summed], project, preferred_element_type=F32)
        ],
        [((rows, width), F32)],
        [update, cyclic, project],
        cost=1000000000,
    )
    for stage in reversed(range(row_stages - 1)):
        got = swap_row(project, [sum_order[stage]] * 2)
        project = got if row_stages == 2 else jnp.concatenate([project, got], 0)
    rest = project if row_stages == 2 else project[summed:]
    return finish(n_row, total, update, rest, summed)


def solution(mesh):
    return jax.shard_map(
        functools.partial(shards, mesh.shape["row"], mesh.shape["col"]),
        mesh=mesh,
        in_specs=(P("row", "col"), P("col"), P("col"), P(), P(), P(), P(None, "row", None), P()),
        out_specs=P("row", "col"),
        check_vma=False,
    )
```

```python
import functools

import jax
import jax.numpy as jnp
from jax import lax
from jax.experimental import pallas as pl
from jax.experimental.pallas import tpu as pltpu
from jax.sharding import PartitionSpec as P

BF = jnp.bfloat16
F32 = jnp.float32
HIGHEST = lax.Precision.HIGHEST
MIB = 2**20


def bit_orders(size, first):
    bits = list(range(first, size.bit_length() - 1))
    half = len(bits) // 2
    return bits, bits[half:] + bits[:half]


def target_codes(bits):
    if not bits:
        return [0]
    rest = target_codes(bits[1:])
    return rest + [(1 << bits[0]) | code for code in rest]


def source_codes(bits):
    codes = [0]
    for bit in bits:
        codes = codes + [(1 << bit) | code for code in codes]
    return codes


def is_even():
    return lax.rem(lax.axis_index("col"), 2) == 0


def select_code(even, pair):
    return pair[0] if pair[0] == pair[1] else jnp.where(even, pair[0], pair[1])


def row_bit(order, stage):
    return jnp.bitwise_and(lax.shift_right_logical(lax.axis_index("row"), order[stage]), 1) == 0


def swap_groups(value, axis, order):
    size = value.shape[axis]
    for stage in range(len(order) - 1):
        step = size >> (stage + 1)
        pieces = [lax.slice_in_dim(value, i, i + step, axis=axis) for i in range(0, size, step)]
        flipped = jnp.concatenate([pieces[i ^ 1] for i in range(len(pieces))], axis)
        value = jnp.where(row_bit(order, stage), value, flipped)
    return value


def local(fn, outs, values, after=(), cost=1):
    outs = [jax.ShapeDtypeStruct(shape, dtype) for shape, dtype in outs]
    if any(v.shape[-1] % 128 or v.shape[-2] % 16 for v in list(values) + outs):
        return list(fn(*values))

    def kernel(*refs):
        ins = refs[:len(values)]
        results = fn(*[ref[...] for ref in ins])
        for ref, result in zip(refs[len(values) + len(after):], results):
            ref[...] = result

    return list(
        pl.pallas_call(
            kernel,
            in_specs=[pl.BlockSpec(memory_space=pltpu.VMEM)] * len(values)
            + [pl.BlockSpec(memory_space=pl.ANY)] * len(after),
            out_specs=[pl.BlockSpec(memory_space=pltpu.VMEM)] * len(outs),
            out_shape=[pltpu.VMEM(o.shape, o.dtype) for o in outs],
            compiler_params=pltpu.CompilerParams(vmem_limit_bytes=16 * MIB),
            cost_estimate=pl.CostEstimate(flops=cost, bytes_accessed=1, transcendentals=0),
        )(*[pltpu.with_memory_space_constraint(v, pltpu.VMEM) for v in values], *after)
    )


def product_kernel(plan, width, chunks, depth, n_after, *refs):
    eig, pole_values, weights, roots, scale = refs[:5]
    outs = refs[5 + n_after:]
    poles = eig.shape[1]
    me = lax.axis_index("col")
    even = is_even()
    piece = width // chunks
    group = max(256 // piece, 1)
    pole_values = pole_values[...]
    weights = weights[...]
    for out, (chunk, codes) in zip(outs, plan):
        for place in range(0, len(codes), group):
            columns = [
                pl.ds(
                    pl.multiple_of(jnp.bitwise_xor(me, select_code(even, pair)) * width + chunk * piece, piece), piece
                )
                for pair in codes[place:place + group]
            ]
            near = jnp.concatenate([roots[:, at] for at in columns], 1)
            near = jnp.concatenate(
                [jnp.broadcast_to(near[:, j:j + 128], (128, 128)).T for j in range(0, near.shape[1], 128)], 0
            )
            total = None
            for k in range(0, poles, depth):
                gaps = pole_values[:, k:k + depth] - jnp.concatenate([near] * (depth // 128), 1)
                matrix = (weights[:, k:k + depth] / gaps).astype(BF)
                term = lax.dot_general(
                    eig[:, k:k + depth], matrix, (((1,), (1,)), ((), ())), preferred_element_type=F32
                )
                total = term if total is None else total + term
            total = total * jnp.concatenate([scale[:, at] for at in columns], 1)
            out[:, place * piece:place * piece + total.shape[1]] = total.astype(BF)


def plain_products(plan, row_codes, parts, chunks, operands):
    eigvecs, pole_order, pole_weight, root_gap, root_shift, column_weight = operands
    poles = eigvecs.shape[1]
    me = lax.axis_index("col")
    places = jnp.bitwise_xor(lax.axis_index("row"), jnp.array(row_codes, jnp.int32))
    ordered = eigvecs.reshape(len(row_codes), -1, poles)[places].reshape(eigvecs.shape)
    results = []
    for chunk, codes in plan:
        places = jnp.array([[a, b] for a, b in codes], jnp.int32)
        places = jnp.bitwise_xor(me, jnp.where(is_even(), places[:, 0], places[:, 1]))
        pick = lambda v: v.reshape(parts, chunks, -1)[places, chunk].reshape(-1)
        root_values = 2.0 * pick(root_gap).astype(F32) + 1.0 + pick(root_shift)
        numer = pole_weight[:, None] * pick(column_weight)[None, :]
        gaps = 2.0 * pole_order.astype(F32)[:, None] - root_values[None, :]
        results.append(jnp.dot(ordered, (numer / gaps).astype(BF), preferred_element_type=F32).astype(BF))
    return results


def products(plan, *, row_codes, parts, chunks, operands, state, after=()):
    rows, poles = operands[0].shape
    width = operands[3].shape[0] // parts
    if state is None:
        return plain_products(plan, row_codes, parts, chunks, operands)
    outs = [pltpu.VMEM((rows, width // chunks * len(codes)), BF) for _, codes in plan]
    return pl.pallas_call(
        functools.partial(product_kernel, plan, width, chunks, poles // 2, len(after)),
        in_specs=[pl.BlockSpec(memory_space=pltpu.VMEM)] * 5 + [pl.BlockSpec(memory_space=pl.ANY)] * len(after),
        out_specs=[pl.BlockSpec(memory_space=pltpu.VMEM)] * len(outs),
        out_shape=outs,
        compiler_params=pltpu.CompilerParams(vmem_limit_bytes=16 * MIB),
        cost_estimate=pl.CostEstimate(flops=1, bytes_accessed=1, transcendentals=0),
    )(*[pltpu.with_memory_space_constraint(operand, pltpu.VMEM) for operand in state], *after)


def panel_kernel(row_codes, row_orders, blocks, *refs):
    eig_hbm, panel_hbm, order_hbm, weight_hbm, gap_hbm, shift_hbm, scale_hbm = refs[:7]
    vectors_out, kept_out, message, correlation_out, eig, pole_values, weights, roots, scales = refs[7:16]
    panel, correlation, order, weight, gap, shift, scale, sem, eig_sem = refs[16:]
    even = is_even()
    row = lax.axis_index("row")
    block = panel.shape[1] // blocks
    targets = list(zip(*[target_codes(order) for order in row_orders]))
    at = lambda code: pl.ds(pl.multiple_of(jnp.bitwise_xor(row, code) * block, block), block)
    copies = [
        pltpu.make_async_copy(src, dst, sem.at[i])
        for i, (src, dst) in enumerate(
            [
                (panel_hbm, panel),
                (order_hbm, order),
                (weight_hbm, weight),
                (gap_hbm, gap),
                (shift_hbm, shift),
                (scale_hbm, scale),
            ]
        )
    ]
    for place, code in enumerate(row_codes):
        copies.append(
            pltpu.make_async_copy(
                eig_hbm.at[at(code)], eig.at[place * block:(place + 1) * block], eig_sem.at[place]
            )
        )
    for copy in copies:
        copy.start()
    for copy in copies[1:6]:
        copy.wait()
    pole_values[...] = (2.0 * order[...].astype(F32)).reshape(pole_values.shape)
    weights[...] = weight[...].reshape(weights.shape)
    roots[...] = (2.0 * gap[...].astype(F32) + 1.0 + shift[...]).reshape(roots.shape)
    scales[...] = scale[...].reshape(scales.shape)
    copies[0].wait()
    for code in range(blocks):
        vectors_out[0, code * block:(code + 1) * block] = panel[0, at(code)]
        vectors_out[1, code * block:(code + 1) * block] = panel[1, at(code)]
    core = jnp.where(even, 0, 1)
    correlation[...] = lax.dot_general(panel[1], panel[0], (((0,), (0,)), ((), ())), preferred_element_type=F32)
    near = correlation_out.shape[0]
    place = lax.shift_right_logical(lax.axis_index("col"), 1)
    part = correlation[pl.ds(pl.multiple_of(place * near, near), near)]
    correlation_out[...] = part
    message[:near] = part.astype(BF)
    for place, pair in enumerate(targets):
        value = panel[core, at(select_code(even, pair))]
        if place < blocks // 2:
            kept_out[place * block:(place + 1) * block] = value
        else:
            start = near + (place - blocks // 2) * block
            message[start:start + block] = value
    for copy in copies[6:]:
        copy.wait()


def panel_blocks(row_codes, row_orders, parts, panel_vectors, operands):
    panels, rows, width = panel_vectors.shape
    blocks = 1 << len(row_orders[0])
    near = width // parts
    poles, roots = operands[1].shape[0], operands[3].shape[0]
    eig_rows = operands[0].shape[0]
    outs = [
        pltpu.VMEM((panels, rows, width), BF),
        pltpu.VMEM((rows // 2, width), BF),
        pltpu.VMEM((near + rows // 2, width), BF),
        pltpu.VMEM((near, width), F32),
        pltpu.VMEM((eig_rows, poles), BF),
        pltpu.VMEM((1, poles), F32),
        pltpu.VMEM((1, poles), F32),
        pltpu.VMEM((1, roots), F32),
        pltpu.VMEM((1, roots), F32),
    ]
    results = pl.pallas_call(
        functools.partial(panel_kernel, row_codes, row_orders, blocks),
        in_specs=[pl.BlockSpec(memory_space=pl.ANY)] * 7,
        out_specs=[pl.BlockSpec(memory_space=pltpu.VMEM)] * len(outs),
        out_shape=outs,
        scratch_shapes=[
            pltpu.VMEM((panels, rows, width), BF),
            pltpu.VMEM((width, width), F32),
            pltpu.VMEM((poles,), jnp.int32),
            pltpu.VMEM((poles,), F32),
            pltpu.VMEM((roots,), jnp.int32),
            pltpu.VMEM((roots,), F32),
            pltpu.VMEM((roots,), F32),
            pltpu.SemaphoreType.DMA((6,)),
            pltpu.SemaphoreType.DMA((blocks,)),
        ],
        compiler_params=pltpu.CompilerParams(vmem_limit_bytes=16 * MIB),
        cost_estimate=pl.CostEstimate(flops=1, bytes_accessed=1, transcendentals=0),
    )(*[pltpu.with_memory_space_constraint(v, pltpu.HBM) for v in (operands[0], panel_vectors, *operands[1:])])
    return results[:4], results[4:]


def finish_kernel(blocks, start, total, update, project, out_hbm, result, sem):
    block = total.shape[0] // blocks
    row = lax.axis_index("row")
    copies = []
    for code in range(blocks):
        rows = slice(code * block, (code + 1) * block)
        value = total[rows] - jnp.dot(update[rows, start:], project[...], preferred_element_type=F32)
        result[rows] = value.astype(BF)
        at = pl.multiple_of(jnp.bitwise_xor(row, code) * block, block)
        copies.append(pltpu.make_async_copy(result.at[rows], out_hbm.at[pl.ds(at, block)], sem.at[code]))
        copies[-1].start()
    for copy in copies:
        copy.wait()


def finish(blocks, total, update, project, start):
    rows, width = total.shape
    if width % 128:
        result = (total - jnp.dot(update[:, start:], project, preferred_element_type=F32)).astype(BF)
        places = jnp.bitwise_xor(lax.axis_index("row"), jnp.arange(blocks))
        return result.reshape(blocks, -1, width)[places].reshape(rows, width)
    return pl.pallas_call(
        functools.partial(finish_kernel, blocks, start),
        in_specs=[pl.BlockSpec(memory_space=pltpu.VMEM)] * 3,
        out_specs=pl.BlockSpec(memory_space=pl.ANY),
        out_shape=jax.ShapeDtypeStruct((rows, width), BF),
        scratch_shapes=[pltpu.VMEM((rows, width), BF), pltpu.SemaphoreType.DMA((blocks,))],
        compiler_params=pltpu.CompilerParams(vmem_limit_bytes=16 * MIB),
        cost_estimate=pl.CostEstimate(flops=1, bytes_accessed=1, transcendentals=0),
    )(*[pltpu.with_memory_space_constraint(v, pltpu.VMEM) for v in (total, update, project)])


def split_dot(left, right):
    def parts(value):
        if value.dtype == BF:
            return [value]
        high = value.astype(BF)
        return [high, (value - high.astype(F32)).astype(BF)]

    total = None
    for i, a in enumerate(parts(left)):
        for j, b in enumerate(parts(right)):
            if i + j < 2:
                term = jnp.dot(a, b, preferred_element_type=F32)
                total = term if total is None else total + term
    return total


def shards(
    n_row,
    n_col,
    eigvecs,
    pole_order,
    pole_weight,
    root_gap,
    root_shift,
    column_weight,
    panel_vectors,
    panel_factors,
):
    col_orders = bit_orders(n_col, 1)
    row_orders = bit_orders(n_row, 0)
    col_stages = len(col_orders[0])
    row_stages = len(row_orders[0])
    rows = eigvecs.shape[0]
    block = rows // n_row
    panel_width = panel_vectors.shape[2]
    parts = n_col // 2
    near = panel_width // parts
    width = root_gap.shape[0] // n_col
    chunks = 2 if width % 256 == 0 else 1
    piece = width // chunks
    sum_order = row_orders[0]
    move_order = sum_order[::-1]

    def swap_cores(value):
        return lax.ppermute(value, "col", [(i, i ^ 1) for i in range(n_col)])

    def swap_col(value, stage):
        return lax.ppermute(value, "col", [(i, i ^ (1 << col_orders[i % 2][stage])) for i in range(n_col)])

    def swap_row(value, bits):
        pairs = [(r * n_col + c, (r ^ (1 << bits[c % 2])) * n_col + c) for r in range(n_row) for c in range(n_col)]
        return lax.ppermute(value, ("row", "col"), pairs)

    def split_targets(value, targets):
        step = targets * block
        kept = [value[i:i + step // 2] for i in range(0, value.shape[0], step)]
        sent = [value[i + step // 2:i + step] for i in range(0, value.shape[0], step)]
        return jnp.concatenate(kept, 0), jnp.concatenate(sent, 0)

    def pick_blocks(value, places):
        return jnp.concatenate([value[i * block:(i + 1) * block] for i in places], 0)

    targets = target_codes(move_order)
    own_codes = list(zip(*[target_codes(order) for order in col_orders]))
    other_codes = [(1 ^ odd, 1 ^ even) for even, odd in own_codes]
    half = len(own_codes) // 2
    operands = (eigvecs, pole_order, pole_weight, root_gap, root_shift, column_weight)
    (vectors, kept, message, correlation), state = panel_blocks(
        targets, row_orders, parts, panel_vectors, operands
    )
    if width % (128 * chunks) or eigvecs.shape[1] % 256:
        state = None
    multiply = functools.partial(
        products, row_codes=targets, parts=n_col, chunks=chunks, operands=operands, state=state
    )
    got_sent, own_sent, made = [], [], ()
    for chunk in range(chunks):
        other, own = multiply([(chunk, other_codes[half:]), (chunk, own_codes[half:])], after=made)
        got_sent.append(swap_cores(other))
        own_sent.append(own)
        made = (own,)
    long = half * piece
    sent = []
    for own, got in zip(own_sent, got_sent):
        (value,) = local(
            lambda own, got: [(own.astype(F32) + got.astype(F32)).astype(BF)],
            [((rows, long), BF)],
            [own, got],
            after=(*made, *sent),
        )
        sent.append(value)
    got = [swap_col(message, 0) for message in sent]
    other_kept = multiply([(chunk, other_codes[:half]) for chunk in range(chunks)], after=(sent[-1],))
    got_kept = [swap_cores(value) for value in other_kept]
    own_kept = multiply([(chunk, own_codes[:half]) for chunk in range(chunks)], after=(other_kept[0],))

    current = [[own, other, new] for own, other, new in zip(own_kept, got_kept, got)]
    for stage in range(1, col_stages):
        long //= 2

        def next_sums(*values, long=long):
            count = len(values) // chunks
            totals = [sum(v.astype(F32) for v in values[i:i + count]) for i in range(0, len(values), count)]
            out = jnp.concatenate([total[:, long:] for total in totals], 1).astype(BF)
            return *[total[:, :long] for total in totals], out

        *totals, col_message = local(
            next_sums,
            [((rows, long), F32)] * chunks + [((rows, chunks * long), BF)],
            sum(current, []),
        )
        if stage == 1:
            first_message = col_message
        got = swap_col(col_message, stage)
        current = [[total, got] for total in totals]
        if stage < col_stages - 1:
            current = [[total, got[:, i * long:(i + 1) * long]] for i, total in enumerate(totals)]

    for stage in range(row_stages):
        panel_got = swap_row(message, [order[stage] for order in row_orders])

        if stage < row_stages - 1:

            def next_panel(kept, correlation, got, targets=n_row >> (stage + 1)):
                correlation = correlation + got[:near].astype(F32)
                kept, moved = split_targets(jnp.concatenate([kept, got[near:]], 0), targets)
                return kept, jnp.concatenate([correlation.astype(BF), moved], 0), correlation

            kept, message, correlation = local(
                next_panel,
                [((rows // 2, panel_width), BF), ((near + rows // 2, panel_width), BF), ((near, panel_width), F32)],
                [kept, correlation, panel_got],
                after=(sent[-1],),
                cost=5000000000,
            )
    panel_places = [[source_codes(order).index(code) for code in range(n_row)] for order in row_orders]

    first_rows = 3 * rows // 4

    def panel_done(kept, correlation, got):
        correlation = (correlation + got[:near].astype(F32)).astype(BF)
        value = jnp.concatenate([kept, got[near:]], 0)
        orders = [pick_blocks(value, places).astype(F32) for places in panel_places]
        value = jnp.where(is_even(), orders[0], orders[1]).astype(BF)
        return value, correlation, value[:first_rows], value[first_rows:]

    mine, correlation, *mine_sent = local(
        panel_done,
        [((r, panel_width), BF) for r in (rows, near, first_rows, rows - first_rows)],
        [kept, correlation, panel_got],
        after=(first_message,),
    )
    other = [swap_cores(value) for value in mine_sent]

    wide = 2 * panel_width
    summed = wide // 2 if row_stages > 1 else wide

    def projections(mine, *values):
        other, values = values[:2], values[2:]
        merged = jnp.concatenate(values[:chunks], 1) + jnp.concatenate(values[chunks:], 1).astype(F32)
        merged = merged.astype(BF)
        dims = (((0,), (0,)), ((), ()))
        project = jnp.concatenate(
            [
                lax.dot_general(pick_blocks(v, targets), merged, dims, preferred_element_type=F32)
                for v in (mine, jnp.concatenate(other, 0))
            ],
            0,
        )
        project = swap_groups(project, 0, sum_order)
        out = project if row_stages == 1 else project[summed:]
        return project[:summed], out.astype(BF), *split_targets(merged, n_row)

    shapes = lambda size: [((size, width), F32), ((size, width), BF)]
    halves = [((rows // 2, width), BF)] * 2
    last_got = [current[0][1]] if col_stages > 1 else [c[1] for c in current]
    project, message, blocks, moved = local(
        projections,
        shapes(summed) + halves,
        [mine, *other, *[c[0] for c in current], *last_got],
    )
    project_got = swap_row(message, [sum_order[0]] * 2)
    blocks_got = swap_row(moved, [move_order[0]] * 2)

    def join(mine, got, stage):
        shift = select_code(is_even(), (col_orders[0][stage], col_orders[1][stage]))
        low = jnp.bitwise_and(lax.shift_right_logical(lax.axis_index("col"), shift), 1) == 0
        mine, got = mine.astype(F32), got.astype(F32)
        return jnp.concatenate([jnp.where(low, mine, got), jnp.where(low, got, mine)], 0)

    joined = near
    for stage in range(col_stages - 1):
        joined *= 2
        (correlation,) = local(
            lambda mine, got, stage=stage: [join(mine, got, stage).astype(BF)],
            [((joined, panel_width), BF)],
            [correlation, swap_col(correlation, stage)],
            after=(message,),
        )
    other_correlation = swap_col(correlation, col_stages - 1)
    part_orders = [source_codes([bit - 1 for bit in order]) for order in col_orders]
    part_orders = [[order.index(part) for part in range(parts)] for order in part_orders]

    def update_factor(vectors, factors, mine, other):
        even = is_even()
        correlation = join(mine, other, col_stages - 1)
        ordered = [
            jnp.concatenate([correlation[i * near:(i + 1) * near] for i in order], 0) for order in part_orders
        ]
        correlation = jnp.where(even, ordered[0], ordered[1]).astype(BF)
        across = split_dot(vectors[1], split_dot(factors[1], correlation))
        first = split_dot(vectors[0].astype(F32) - across, factors[0])
        second = split_dot(vectors[1], factors[1])
        update = jnp.concatenate([jnp.where(even, first, second), jnp.where(even, second, first)], 1)
        return [swap_groups(update, 1, sum_order).astype(BF)]

    for stage in range(1, row_stages):
        last = stage == row_stages - 1
        size = summed if last else summed // 2

        def next_project(project, got, last=last, size=size):
            total = project + got.astype(F32)
            return total[:size], (total if last else total[size:]).astype(BF)

        project, message = local(
            next_project, shapes(size), [project, project_got], after=(correlation,) if stage == 1 else ()
        )
        project_got = swap_row(message, [sum_order[stage]] * 2)
        summed = size
    (update,) = local(
        update_factor,
        [((rows, wide), BF)],
        [vectors, panel_factors, correlation, other_correlation],
        after=(message,),
        cost=1000000000,
    )

    for stage in range(1, row_stages):
        blocks, moved = local(
            lambda blocks, got, targets=n_row >> stage: split_targets(jnp.concatenate([blocks, got], 0), targets),
            halves,
            [blocks, blocks_got],
        )
        blocks_got = swap_row(moved, [move_order[stage]] * 2)
    move_places = [source_codes(move_order).index(code) for code in range(n_row)]
    (cyclic,) = local(
        lambda blocks, got: [pick_blocks(jnp.concatenate([blocks, got], 0), move_places)],
        [((rows, width), BF)],
        [blocks, blocks_got],
    )
    (project,) = local(
        lambda project, got: [(project + got.astype(F32)).astype(BF)],
        [((summed, width), BF)],
        [project, project_got],
    )
    (total,) = local(
        lambda update, cyclic, project: [
            cyclic.astype(F32) - jnp.dot(update[:, :summed], project, preferred_element_type=F32)
        ],
        [((rows, width), F32)],
        [update, cyclic, project],
        cost=1000000000,
    )
    for stage in reversed(range(row_stages - 1)):
        got = swap_row(project, [sum_order[stage]] * 2)
        project = got if row_stages == 2 else jnp.concatenate([project, got], 0)
    rest = project if row_stages == 2 else project[summed:]
    return finish(n_row, total, update, rest, summed)


def solution(mesh):
    return jax.shard_map(
        functools.partial(shards, mesh.shape["row"], mesh.shape["col"]),
        mesh=mesh,
        in_specs=(P("row", "col"), P("col"), P("col"), P(), P(), P(), P(None, "row", None), P()),
        out_specs=P("row", "col"),
        check_vma=False,
    )
```

```python
import functools

import jax
import jax.numpy as jnp
from jax import lax
from jax.experimental import pallas as pl
from jax.experimental.pallas import tpu as pltpu
from jax.sharding import PartitionSpec as P

BF = jnp.bfloat16
F32 = jnp.float32
HIGHEST = lax.Precision.HIGHEST
MIB = 2**20


def bit_orders(size, first):
    bits = list(range(first, size.bit_length() - 1))
    half = len(bits) // 2
    return bits, bits[half:] + bits[:half]


def target_codes(bits):
    if not bits:
        return [0]
    rest = target_codes(bits[1:])
    return rest + [(1 << bits[0]) | code for code in rest]


def source_codes(bits):
    codes = [0]
    for bit in bits:
        codes = codes + [(1 << bit) | code for code in codes]
    return codes


def is_even():
    return lax.rem(lax.axis_index("col"), 2) == 0


def select_code(even, pair):
    return pair[0] if pair[0] == pair[1] else jnp.where(even, pair[0], pair[1])


def row_bit(order, stage):
    return jnp.bitwise_and(lax.shift_right_logical(lax.axis_index("row"), order[stage]), 1) == 0


def swap_groups(value, axis, order):
    size = value.shape[axis]
    for stage in range(len(order) - 1):
        step = size >> (stage + 1)
        pieces = [lax.slice_in_dim(value, i, i + step, axis=axis) for i in range(0, size, step)]
        flipped = jnp.concatenate([pieces[i ^ 1] for i in range(len(pieces))], axis)
        value = jnp.where(row_bit(order, stage), value, flipped)
    return value


def local(fn, outs, values, after=(), cost=1):
    outs = [jax.ShapeDtypeStruct(shape, dtype) for shape, dtype in outs]
    if any(v.shape[-1] % 128 or v.shape[-2] % 16 for v in list(values) + outs):
        return list(fn(*values))

    def kernel(*refs):
        ins = refs[:len(values)]
        results = fn(*[ref[...] for ref in ins])
        for ref, result in zip(refs[len(values) + len(after):], results):
            ref[...] = result

    return list(
        pl.pallas_call(
            kernel,
            in_specs=[pl.BlockSpec(memory_space=pltpu.VMEM)] * len(values)
            + [pl.BlockSpec(memory_space=pl.ANY)] * len(after),
            out_specs=[pl.BlockSpec(memory_space=pltpu.VMEM)] * len(outs),
            out_shape=[pltpu.VMEM(o.shape, o.dtype) for o in outs],
            compiler_params=pltpu.CompilerParams(vmem_limit_bytes=16 * MIB),
            cost_estimate=pl.CostEstimate(flops=cost, bytes_accessed=1, transcendentals=0),
        )(*[pltpu.with_memory_space_constraint(v, pltpu.VMEM) for v in values], *after)
    )


def product_kernel(plan, width, chunks, depth, n_after, *refs):
    eig, pole_values, weights, roots, scale = refs[:5]
    outs = refs[5 + n_after:]
    poles = eig.shape[1]
    me = lax.axis_index("col")
    even = is_even()
    piece = width // chunks
    group = max(256 // piece, 1)
    pole_values = pole_values[...]
    weights = weights[...]
    for out, (chunk, codes) in zip(outs, plan):
        for place in range(0, len(codes), group):
            columns = [
                pl.ds(
                    pl.multiple_of(jnp.bitwise_xor(me, select_code(even, pair)) * width + chunk * piece, piece), piece
                )
                for pair in codes[place:place + group]
            ]
            near = jnp.concatenate([roots[:, at] for at in columns], 1)
            near = jnp.concatenate(
                [jnp.broadcast_to(near[:, j:j + 128], (128, 128)).T for j in range(0, near.shape[1], 128)], 0
            )
            total = None
            for k in range(0, poles, depth):
                gaps = pole_values[:, k:k + depth] - jnp.concatenate([near] * (depth // 128), 1)
                matrix = (weights[:, k:k + depth] / gaps).astype(BF)
                term = lax.dot_general(
                    eig[:, k:k + depth], matrix, (((1,), (1,)), ((), ())), preferred_element_type=F32
                )
                total = term if total is None else total + term
            total = total * jnp.concatenate([scale[:, at] for at in columns], 1)
            out[:, place * piece:place * piece + total.shape[1]] = total.astype(BF)


def plain_products(plan, row_codes, parts, chunks, operands):
    eigvecs, pole_order, pole_weight, root_gap, root_shift, column_weight = operands
    poles = eigvecs.shape[1]
    me = lax.axis_index("col")
    places = jnp.bitwise_xor(lax.axis_index("row"), jnp.array(row_codes, jnp.int32))
    ordered = eigvecs.reshape(len(row_codes), -1, poles)[places].reshape(eigvecs.shape)
    results = []
    for chunk, codes in plan:
        places = jnp.array([[a, b] for a, b in codes], jnp.int32)
        places = jnp.bitwise_xor(me, jnp.where(is_even(), places[:, 0], places[:, 1]))
        pick = lambda v: v.reshape(parts, chunks, -1)[places, chunk].reshape(-1)
        root_values = 2.0 * pick(root_gap).astype(F32) + 1.0 + pick(root_shift)
        numer = pole_weight[:, None] * pick(column_weight)[None, :]
        gaps = 2.0 * pole_order.astype(F32)[:, None] - root_values[None, :]
        results.append(jnp.dot(ordered, (numer / gaps).astype(BF), preferred_element_type=F32).astype(BF))
    return results


def products(plan, *, row_codes, parts, chunks, operands, state, after=()):
    rows, poles = operands[0].shape
    width = operands[3].shape[0] // parts
    if state is None:
        return plain_products(plan, row_codes, parts, chunks, operands)
    outs = [pltpu.VMEM((rows, width // chunks * len(codes)), BF) for _, codes in plan]
    return pl.pallas_call(
        functools.partial(product_kernel, plan, width, chunks, poles // 2, len(after)),
        in_specs=[pl.BlockSpec(memory_space=pltpu.VMEM)] * 5 + [pl.BlockSpec(memory_space=pl.ANY)] * len(after),
        out_specs=[pl.BlockSpec(memory_space=pltpu.VMEM)] * len(outs),
        out_shape=outs,
        compiler_params=pltpu.CompilerParams(vmem_limit_bytes=16 * MIB),
        cost_estimate=pl.CostEstimate(flops=1, bytes_accessed=1, transcendentals=0),
    )(*[pltpu.with_memory_space_constraint(operand, pltpu.VMEM) for operand in state], *after)


def panel_kernel(row_codes, row_orders, blocks, *refs):
    eig_hbm, panel_hbm, order_hbm, weight_hbm, gap_hbm, shift_hbm, scale_hbm = refs[:7]
    vectors_out, kept_out, message, correlation_out, eig, pole_values, weights, roots, scales = refs[7:16]
    panel, correlation, order, weight, gap, shift, scale, sem, eig_sem = refs[16:]
    even = is_even()
    row = lax.axis_index("row")
    block = panel.shape[1] // blocks
    targets = list(zip(*[target_codes(order) for order in row_orders]))
    at = lambda code: pl.ds(pl.multiple_of(jnp.bitwise_xor(row, code) * block, block), block)
    copies = [
        pltpu.make_async_copy(src, dst, sem.at[i])
        for i, (src, dst) in enumerate(
            [
                (panel_hbm, panel),
                (order_hbm, order),
                (weight_hbm, weight),
                (gap_hbm, gap),
                (shift_hbm, shift),
                (scale_hbm, scale),
            ]
        )
    ]
    for place, code in enumerate(row_codes):
        copies.append(
            pltpu.make_async_copy(
                eig_hbm.at[at(code)], eig.at[place * block:(place + 1) * block], eig_sem.at[place]
            )
        )
    for copy in copies:
        copy.start()
    for copy in copies[1:6]:
        copy.wait()
    pole_values[...] = (2.0 * order[...].astype(F32)).reshape(pole_values.shape)
    weights[...] = weight[...].reshape(weights.shape)
    roots[...] = (2.0 * gap[...].astype(F32) + 1.0 + shift[...]).reshape(roots.shape)
    scales[...] = scale[...].reshape(scales.shape)
    copies[0].wait()
    for code in range(blocks):
        vectors_out[0, code * block:(code + 1) * block] = panel[0, at(code)]
        vectors_out[1, code * block:(code + 1) * block] = panel[1, at(code)]
    core = jnp.where(even, 0, 1)
    correlation[...] = lax.dot_general(panel[1], panel[0], (((0,), (0,)), ((), ())), preferred_element_type=F32)
    near = correlation_out.shape[0]
    place = lax.shift_right_logical(lax.axis_index("col"), 1)
    part = correlation[pl.ds(pl.multiple_of(place * near, near), near)]
    correlation_out[...] = part
    message[:near] = part.astype(BF)
    for place, pair in enumerate(targets):
        value = panel[core, at(select_code(even, pair))]
        if place < blocks // 2:
            kept_out[place * block:(place + 1) * block] = value
        else:
            start = near + (place - blocks // 2) * block
            message[start:start + block] = value
    for copy in copies[6:]:
        copy.wait()


def panel_blocks(row_codes, row_orders, parts, panel_vectors, operands):
    panels, rows, width = panel_vectors.shape
    blocks = 1 << len(row_orders[0])
    near = width // parts
    poles, roots = operands[1].shape[0], operands[3].shape[0]
    eig_rows = operands[0].shape[0]
    outs = [
        pltpu.VMEM((panels, rows, width), BF),
        pltpu.VMEM((rows // 2, width), BF),
        pltpu.VMEM((near + rows // 2, width), BF),
        pltpu.VMEM((near, width), F32),
        pltpu.VMEM((eig_rows, poles), BF),
        pltpu.VMEM((1, poles), F32),
        pltpu.VMEM((1, poles), F32),
        pltpu.VMEM((1, roots), F32),
        pltpu.VMEM((1, roots), F32),
    ]
    results = pl.pallas_call(
        functools.partial(panel_kernel, row_codes, row_orders, blocks),
        in_specs=[pl.BlockSpec(memory_space=pl.ANY)] * 7,
        out_specs=[pl.BlockSpec(memory_space=pltpu.VMEM)] * len(outs),
        out_shape=outs,
        scratch_shapes=[
            pltpu.VMEM((panels, rows, width), BF),
            pltpu.VMEM((width, width), F32),
            pltpu.VMEM((poles,), jnp.int32),
            pltpu.VMEM((poles,), F32),
            pltpu.VMEM((roots,), jnp.int32),
            pltpu.VMEM((roots,), F32),
            pltpu.VMEM((roots,), F32),
            pltpu.SemaphoreType.DMA((6,)),
            pltpu.SemaphoreType.DMA((blocks,)),
        ],
        compiler_params=pltpu.CompilerParams(vmem_limit_bytes=16 * MIB),
        cost_estimate=pl.CostEstimate(flops=1, bytes_accessed=1, transcendentals=0),
    )(*[pltpu.with_memory_space_constraint(v, pltpu.HBM) for v in (operands[0], panel_vectors, *operands[1:])])
    return results[:4], results[4:]


def finish_kernel(blocks, start, total, update, project, out_hbm, result, sem):
    block = total.shape[0] // blocks
    row = lax.axis_index("row")
    copies = []
    for code in range(blocks):
        rows = slice(code * block, (code + 1) * block)
        value = total[rows] - jnp.dot(update[rows, start:], project[...], preferred_element_type=F32)
        result[rows] = value.astype(BF)
        at = pl.multiple_of(jnp.bitwise_xor(row, code) * block, block)
        copies.append(pltpu.make_async_copy(result.at[rows], out_hbm.at[pl.ds(at, block)], sem.at[code]))
        copies[-1].start()
    for copy in copies:
        copy.wait()


def finish(blocks, total, update, project, start):
    rows, width = total.shape
    if width % 128:
        result = (total - jnp.dot(update[:, start:], project, preferred_element_type=F32)).astype(BF)
        places = jnp.bitwise_xor(lax.axis_index("row"), jnp.arange(blocks))
        return result.reshape(blocks, -1, width)[places].reshape(rows, width)
    return pl.pallas_call(
        functools.partial(finish_kernel, blocks, start),
        in_specs=[pl.BlockSpec(memory_space=pltpu.VMEM)] * 3,
        out_specs=pl.BlockSpec(memory_space=pl.ANY),
        out_shape=jax.ShapeDtypeStruct((rows, width), BF),
        scratch_shapes=[pltpu.VMEM((rows, width), BF), pltpu.SemaphoreType.DMA((blocks,))],
        compiler_params=pltpu.CompilerParams(vmem_limit_bytes=16 * MIB),
        cost_estimate=pl.CostEstimate(flops=1, bytes_accessed=1, transcendentals=0),
    )(*[pltpu.with_memory_space_constraint(v, pltpu.VMEM) for v in (total, update, project)])


def split_dot(left, right):
    def parts(value):
        if value.dtype == BF:
            return [value]
        high = value.astype(BF)
        return [high, (value - high.astype(F32)).astype(BF)]

    total = None
    for i, a in enumerate(parts(left)):
        for j, b in enumerate(parts(right)):
            if i + j < 2:
                term = jnp.dot(a, b, preferred_element_type=F32)
                total = term if total is None else total + term
    return total


def shards(
    n_row,
    n_col,
    eigvecs,
    pole_order,
    pole_weight,
    root_gap,
    root_shift,
    column_weight,
    panel_vectors,
    panel_factors,
):
    col_orders = bit_orders(n_col, 1)[::-1]
    row_orders = bit_orders(n_row, 0)
    col_stages = len(col_orders[0])
    row_stages = len(row_orders[0])
    rows = eigvecs.shape[0]
    block = rows // n_row
    panel_width = panel_vectors.shape[2]
    parts = n_col // 2
    near = panel_width // parts
    width = root_gap.shape[0] // n_col
    chunks = 2 if width % 256 == 0 else 1
    piece = width // chunks
    sum_order = row_orders[0]
    move_order = sum_order[::-1]

    def swap_cores(value):
        return lax.ppermute(value, "col", [(i, i ^ 1) for i in range(n_col)])

    def swap_col(value, stage):
        return lax.ppermute(value, "col", [(i, i ^ (1 << col_orders[i % 2][stage])) for i in range(n_col)])

    def swap_row(value, bits):
        pairs = [(r * n_col + c, (r ^ (1 << bits[c % 2])) * n_col + c) for r in range(n_row) for c in range(n_col)]
        return lax.ppermute(value, ("row", "col"), pairs)

    def split_targets(value, targets):
        step = targets * block
        kept = [value[i:i + step // 2] for i in range(0, value.shape[0], step)]
        sent = [value[i + step // 2:i + step] for i in range(0, value.shape[0], step)]
        return jnp.concatenate(kept, 0), jnp.concatenate(sent, 0)

    def pick_blocks(value, places):
        return jnp.concatenate([value[i * block:(i + 1) * block] for i in places], 0)

    targets = target_codes(move_order)
    own_codes = list(zip(*[target_codes(order) for order in col_orders]))
    other_codes = [(1 ^ odd, 1 ^ even) for even, odd in own_codes]
    half = len(own_codes) // 2
    operands = (eigvecs, pole_order, pole_weight, root_gap, root_shift, column_weight)
    (vectors, kept, message, correlation), state = panel_blocks(
        targets, row_orders, parts, panel_vectors, operands
    )
    if width % (128 * chunks) or eigvecs.shape[1] % 256:
        state = None
    multiply = functools.partial(
        products, row_codes=targets, parts=n_col, chunks=chunks, operands=operands, state=state
    )
    got_sent, own_sent, made = [], [], ()
    for chunk in range(chunks):
        other, own = multiply([(chunk, other_codes[half:]), (chunk, own_codes[half:])], after=made)
        got_sent.append(swap_cores(other))
        own_sent.append(own)
        made = (own,)
    long = half * piece
    sent = []
    for own, got in zip(own_sent, got_sent):
        (value,) = local(
            lambda own, got: [(own.astype(F32) + got.astype(F32)).astype(BF)],
            [((rows, long), BF)],
            [own, got],
            after=(*made, *sent),
        )
        sent.append(value)
    got = [swap_col(message, 0) for message in sent]
    other_kept = multiply([(chunk, other_codes[:half]) for chunk in range(chunks)], after=(sent[-1],))
    got_kept = [swap_cores(value) for value in other_kept]
    own_kept = multiply([(chunk, own_codes[:half]) for chunk in range(chunks)], after=(other_kept[0],))

    current = [[own, other, new] for own, other, new in zip(own_kept, got_kept, got)]
    for stage in range(1, col_stages):
        long //= 2

        def next_sums(*values, long=long):
            count = len(values) // chunks
            totals = [sum(v.astype(F32) for v in values[i:i + count]) for i in range(0, len(values), count)]
            out = jnp.concatenate([total[:, long:] for total in totals], 1).astype(BF)
            return *[total[:, :long] for total in totals], out

        *totals, col_message = local(
            next_sums,
            [((rows, long), F32)] * chunks + [((rows, chunks * long), BF)],
            sum(current, []),
        )
        if stage == 1:
            first_message = col_message
        got = swap_col(col_message, stage)
        current = [[total, got] for total in totals]
        if stage < col_stages - 1:
            current = [[total, got[:, i * long:(i + 1) * long]] for i, total in enumerate(totals)]

    for stage in range(row_stages):
        panel_got = swap_row(message, [order[stage] for order in row_orders])

        if stage < row_stages - 1:

            def next_panel(kept, correlation, got, targets=n_row >> (stage + 1)):
                correlation = correlation + got[:near].astype(F32)
                kept, moved = split_targets(jnp.concatenate([kept, got[near:]], 0), targets)
                return kept, jnp.concatenate([correlation.astype(BF), moved], 0), correlation

            kept, message, correlation = local(
                next_panel,
                [((rows // 2, panel_width), BF), ((near + rows // 2, panel_width), BF), ((near, panel_width), F32)],
                [kept, correlation, panel_got],
                after=(sent[-1],),
                cost=5000000000,
            )
    panel_places = [[source_codes(order).index(code) for code in range(n_row)] for order in row_orders]

    first_rows = 3 * rows // 4

    def panel_done(kept, correlation, got):
        correlation = (correlation + got[:near].astype(F32)).astype(BF)
        value = jnp.concatenate([kept, got[near:]], 0)
        orders = [pick_blocks(value, places).astype(F32) for places in panel_places]
        value = jnp.where(is_even(), orders[0], orders[1]).astype(BF)
        return value, correlation, value[:first_rows], value[first_rows:]

    mine, correlation, *mine_sent = local(
        panel_done,
        [((r, panel_width), BF) for r in (rows, near, first_rows, rows - first_rows)],
        [kept, correlation, panel_got],
        after=(first_message,),
    )
    other = [swap_cores(value) for value in mine_sent]

    wide = 2 * panel_width
    summed = wide // 2 if row_stages > 1 else wide

    def projections(mine, *values):
        other, values = values[:2], values[2:]
        merged = jnp.concatenate(values[:chunks], 1) + jnp.concatenate(values[chunks:], 1).astype(F32)
        merged = merged.astype(BF)
        dims = (((0,), (0,)), ((), ()))
        project = jnp.concatenate(
            [
                lax.dot_general(pick_blocks(v, targets), merged, dims, preferred_element_type=F32)
                for v in (mine, jnp.concatenate(other, 0))
            ],
            0,
        )
        project = swap_groups(project, 0, sum_order)
        out = project if row_stages == 1 else project[summed:]
        return project[:summed], out.astype(BF), *split_targets(merged, n_row)

    shapes = lambda size: [((size, width), F32), ((size, width), BF)]
    halves = [((rows // 2, width), BF)] * 2
    last_got = [current[0][1]] if col_stages > 1 else [c[1] for c in current]
    project, message, blocks, moved = local(
        projections,
        shapes(summed) + halves,
        [mine, *other, *[c[0] for c in current], *last_got],
    )
    project_got = swap_row(message, [sum_order[0]] * 2)
    blocks_got = swap_row(moved, [move_order[0]] * 2)

    def join(mine, got, stage):
        shift = select_code(is_even(), (col_orders[0][stage], col_orders[1][stage]))
        low = jnp.bitwise_and(lax.shift_right_logical(lax.axis_index("col"), shift), 1) == 0
        mine, got = mine.astype(F32), got.astype(F32)
        return jnp.concatenate([jnp.where(low, mine, got), jnp.where(low, got, mine)], 0)

    joined = near
    for stage in range(col_stages - 1):
        joined *= 2
        (correlation,) = local(
            lambda mine, got, stage=stage: [join(mine, got, stage).astype(BF)],
            [((joined, panel_width), BF)],
            [correlation, swap_col(correlation, stage)],
            after=(message,),
        )
    other_correlation = swap_col(correlation, col_stages - 1)
    part_orders = [source_codes([bit - 1 for bit in order]) for order in col_orders]
    part_orders = [[order.index(part) for part in range(parts)] for order in part_orders]

    def update_factor(vectors, factors, mine, other):
        even = is_even()
        correlation = join(mine, other, col_stages - 1)
        ordered = [
            jnp.concatenate([correlation[i * near:(i + 1) * near] for i in order], 0) for order in part_orders
        ]
        correlation = jnp.where(even, ordered[0], ordered[1]).astype(BF)
        across = split_dot(vectors[1], split_dot(factors[1], correlation))
        first = split_dot(vectors[0].astype(F32) - across, factors[0])
        second = split_dot(vectors[1], factors[1])
        update = jnp.concatenate([jnp.where(even, first, second), jnp.where(even, second, first)], 1)
        return [swap_groups(update, 1, sum_order).astype(BF)]

    for stage in range(1, row_stages):
        last = stage == row_stages - 1
        size = summed if last else summed // 2

        def next_project(project, got, last=last, size=size):
            total = project + got.astype(F32)
            return total[:size], (total if last else total[size:]).astype(BF)

        project, message = local(
            next_project, shapes(size), [project, project_got], after=(correlation,) if stage == 1 else ()
        )
        project_got = swap_row(message, [sum_order[stage]] * 2)
        summed = size
    (update,) = local(
        update_factor,
        [((rows, wide), BF)],
        [vectors, panel_factors, correlation, other_correlation],
        after=(message,),
        cost=1000000000,
    )

    for stage in range(1, row_stages):
        blocks, moved = local(
            lambda blocks, got, targets=n_row >> stage: split_targets(jnp.concatenate([blocks, got], 0), targets),
            halves,
            [blocks, blocks_got],
        )
        blocks_got = swap_row(moved, [move_order[stage]] * 2)
    move_places = [source_codes(move_order).index(code) for code in range(n_row)]
    (cyclic,) = local(
        lambda blocks, got: [pick_blocks(jnp.concatenate([blocks, got], 0), move_places)],
        [((rows, width), BF)],
        [blocks, blocks_got],
    )
    (project,) = local(
        lambda project, got: [(project + got.astype(F32)).astype(BF)],
        [((summed, width), BF)],
        [project, project_got],
    )
    (total,) = local(
        lambda update, cyclic, project: [
            cyclic.astype(F32) - jnp.dot(update[:, :summed], project, preferred_element_type=F32)
        ],
        [((rows, width), F32)],
        [update, cyclic, project],
        cost=1000000000,
    )
    for stage in reversed(range(row_stages - 1)):
        got = swap_row(project, [sum_order[stage]] * 2)
        project = got if row_stages == 2 else jnp.concatenate([project, got], 0)
    rest = project if row_stages == 2 else project[summed:]
    return finish(n_row, total, update, rest, summed)


def solution(mesh):
    return jax.shard_map(
        functools.partial(shards, mesh.shape["row"], mesh.shape["col"]),
        mesh=mesh,
        in_specs=(P("row", "col"), P("col"), P("col"), P(), P(), P(), P(None, "row", None), P()),
        out_specs=P("row", "col"),
        check_vma=False,
    )
```

```python
import functools

import jax
import jax.numpy as jnp
from jax import lax
from jax.experimental import pallas as pl
from jax.experimental.pallas import tpu as pltpu
from jax.sharding import PartitionSpec as P

BF = jnp.bfloat16
F32 = jnp.float32
HIGHEST = lax.Precision.HIGHEST
MIB = 2**20


def bit_orders(size, first):
    bits = list(range(first, size.bit_length() - 1))
    half = len(bits) // 2
    return bits, bits[half:] + bits[:half]


def target_codes(bits):
    if not bits:
        return [0]
    rest = target_codes(bits[1:])
    return rest + [(1 << bits[0]) | code for code in rest]


def source_codes(bits):
    codes = [0]
    for bit in bits:
        codes = codes + [(1 << bit) | code for code in codes]
    return codes


def is_even():
    return lax.rem(lax.axis_index("col"), 2) == 0


def select_code(even, pair):
    return pair[0] if pair[0] == pair[1] else jnp.where(even, pair[0], pair[1])


def row_bit(order, stage):
    return jnp.bitwise_and(lax.shift_right_logical(lax.axis_index("row"), order[stage]), 1) == 0


def swap_groups(value, axis, order):
    size = value.shape[axis]
    for stage in range(len(order) - 1):
        step = size >> (stage + 1)
        pieces = [lax.slice_in_dim(value, i, i + step, axis=axis) for i in range(0, size, step)]
        flipped = jnp.concatenate([pieces[i ^ 1] for i in range(len(pieces))], axis)
        value = jnp.where(row_bit(order, stage), value, flipped)
    return value


def local(fn, outs, values, after=(), cost=1):
    outs = [jax.ShapeDtypeStruct(shape, dtype) for shape, dtype in outs]
    if any(v.shape[-1] % 128 or v.shape[-2] % 16 for v in list(values) + outs):
        return list(fn(*values))

    def kernel(*refs):
        ins = refs[:len(values)]
        results = fn(*[ref[...] for ref in ins])
        for ref, result in zip(refs[len(values) + len(after):], results):
            ref[...] = result

    return list(
        pl.pallas_call(
            kernel,
            in_specs=[pl.BlockSpec(memory_space=pltpu.VMEM)] * len(values)
            + [pl.BlockSpec(memory_space=pl.ANY)] * len(after),
            out_specs=[pl.BlockSpec(memory_space=pltpu.VMEM)] * len(outs),
            out_shape=[pltpu.VMEM(o.shape, o.dtype) for o in outs],
            compiler_params=pltpu.CompilerParams(vmem_limit_bytes=16 * MIB),
            cost_estimate=pl.CostEstimate(flops=cost, bytes_accessed=1, transcendentals=0),
        )(*[pltpu.with_memory_space_constraint(v, pltpu.VMEM) for v in values], *after)
    )


def product_kernel(plan, width, chunks, depth, n_after, *refs):
    eig, pole_values, weights, roots, scale = refs[:5]
    outs = refs[5 + n_after:]
    poles = eig.shape[1]
    me = lax.axis_index("col")
    even = is_even()
    piece = width // chunks
    group = max(256 // piece, 1)
    pole_values = pole_values[...]
    weights = weights[...]
    for out, (chunk, codes) in zip(outs, plan):
        for place in range(0, len(codes), group):
            columns = [
                pl.ds(
                    pl.multiple_of(jnp.bitwise_xor(me, select_code(even, pair)) * width + chunk * piece, piece), piece
                )
                for pair in codes[place:place + group]
            ]
            near = jnp.concatenate([roots[:, at] for at in columns], 1)
            near = jnp.concatenate(
                [jnp.broadcast_to(near[:, j:j + 128], (128, 128)).T for j in range(0, near.shape[1], 128)], 0
            )
            total = None
            for k in range(0, poles, depth):
                gaps = pole_values[:, k:k + depth] - jnp.concatenate([near] * (depth // 128), 1)
                matrix = (weights[:, k:k + depth] / gaps).astype(BF)
                term = lax.dot_general(
                    eig[:, k:k + depth], matrix, (((1,), (1,)), ((), ())), preferred_element_type=F32
                )
                total = term if total is None else total + term
            total = total * jnp.concatenate([scale[:, at] for at in columns], 1)
            out[:, place * piece:place * piece + total.shape[1]] = total.astype(BF)


def plain_products(plan, row_codes, parts, chunks, operands):
    eigvecs, pole_order, pole_weight, root_gap, root_shift, column_weight = operands
    poles = eigvecs.shape[1]
    me = lax.axis_index("col")
    places = jnp.bitwise_xor(lax.axis_index("row"), jnp.array(row_codes, jnp.int32))
    ordered = eigvecs.reshape(len(row_codes), -1, poles)[places].reshape(eigvecs.shape)
    results = []
    for chunk, codes in plan:
        places = jnp.array([[a, b] for a, b in codes], jnp.int32)
        places = jnp.bitwise_xor(me, jnp.where(is_even(), places[:, 0], places[:, 1]))
        pick = lambda v: v.reshape(parts, chunks, -1)[places, chunk].reshape(-1)
        root_values = 2.0 * pick(root_gap).astype(F32) + 1.0 + pick(root_shift)
        numer = pole_weight[:, None] * pick(column_weight)[None, :]
        gaps = 2.0 * pole_order.astype(F32)[:, None] - root_values[None, :]
        results.append(jnp.dot(ordered, (numer / gaps).astype(BF), preferred_element_type=F32).astype(BF))
    return results


def products(plan, *, row_codes, parts, chunks, operands, state, after=()):
    rows, poles = operands[0].shape
    width = operands[3].shape[0] // parts
    if state is None:
        return plain_products(plan, row_codes, parts, chunks, operands)
    outs = [pltpu.VMEM((rows, width // chunks * len(codes)), BF) for _, codes in plan]
    return pl.pallas_call(
        functools.partial(product_kernel, plan, width, chunks, poles, len(after)),
        in_specs=[pl.BlockSpec(memory_space=pltpu.VMEM)] * 5 + [pl.BlockSpec(memory_space=pl.ANY)] * len(after),
        out_specs=[pl.BlockSpec(memory_space=pltpu.VMEM)] * len(outs),
        out_shape=outs,
        compiler_params=pltpu.CompilerParams(vmem_limit_bytes=16 * MIB),
        cost_estimate=pl.CostEstimate(flops=1, bytes_accessed=1, transcendentals=0),
    )(*[pltpu.with_memory_space_constraint(operand, pltpu.VMEM) for operand in state], *after)


def panel_kernel(row_codes, row_orders, blocks, *refs):
    eig_hbm, panel_hbm, order_hbm, weight_hbm, gap_hbm, shift_hbm, scale_hbm = refs[:7]
    vectors_out, kept_out, message, correlation_out, eig, pole_values, weights, roots, scales = refs[7:16]
    panel, correlation, order, weight, gap, shift, scale, sem, eig_sem = refs[16:]
    even = is_even()
    row = lax.axis_index("row")
    block = panel.shape[1] // blocks
    targets = list(zip(*[target_codes(order) for order in row_orders]))
    at = lambda code: pl.ds(pl.multiple_of(jnp.bitwise_xor(row, code) * block, block), block)
    copies = [
        pltpu.make_async_copy(src, dst, sem.at[i])
        for i, (src, dst) in enumerate(
            [
                (panel_hbm, panel),
                (order_hbm, order),
                (weight_hbm, weight),
                (gap_hbm, gap),
                (shift_hbm, shift),
                (scale_hbm, scale),
            ]
        )
    ]
    for place, code in enumerate(row_codes):
        copies.append(
            pltpu.make_async_copy(
                eig_hbm.at[at(code)], eig.at[place * block:(place + 1) * block], eig_sem.at[place]
            )
        )
    for copy in copies:
        copy.start()
    for copy in copies[1:6]:
        copy.wait()
    pole_values[...] = (2.0 * order[...].astype(F32)).reshape(pole_values.shape)
    weights[...] = weight[...].reshape(weights.shape)
    roots[...] = (2.0 * gap[...].astype(F32) + 1.0 + shift[...]).reshape(roots.shape)
    scales[...] = scale[...].reshape(scales.shape)
    copies[0].wait()
    for code in range(blocks):
        vectors_out[0, code * block:(code + 1) * block] = panel[0, at(code)]
        vectors_out[1, code * block:(code + 1) * block] = panel[1, at(code)]
    core = jnp.where(even, 0, 1)
    correlation[...] = lax.dot_general(panel[1], panel[0], (((0,), (0,)), ((), ())), preferred_element_type=F32)
    near = correlation_out.shape[0]
    place = lax.shift_right_logical(lax.axis_index("col"), 1)
    part = correlation[pl.ds(pl.multiple_of(place * near, near), near)]
    correlation_out[...] = part
    message[:near] = part.astype(BF)
    for place, pair in enumerate(targets):
        value = panel[core, at(select_code(even, pair))]
        if place < blocks // 2:
            kept_out[place * block:(place + 1) * block] = value
        else:
            start = near + (place - blocks // 2) * block
            message[start:start + block] = value
    for copy in copies[6:]:
        copy.wait()


def panel_blocks(row_codes, row_orders, parts, panel_vectors, operands):
    panels, rows, width = panel_vectors.shape
    blocks = 1 << len(row_orders[0])
    near = width // parts
    poles, roots = operands[1].shape[0], operands[3].shape[0]
    eig_rows = operands[0].shape[0]
    outs = [
        pltpu.VMEM((panels, rows, width), BF),
        pltpu.VMEM((rows // 2, width), BF),
        pltpu.VMEM((near + rows // 2, width), BF),
        pltpu.VMEM((near, width), F32),
        pltpu.VMEM((eig_rows, poles), BF),
        pltpu.VMEM((1, poles), F32),
        pltpu.VMEM((1, poles), F32),
        pltpu.VMEM((1, roots), F32),
        pltpu.VMEM((1, roots), F32),
    ]
    results = pl.pallas_call(
        functools.partial(panel_kernel, row_codes, row_orders, blocks),
        in_specs=[pl.BlockSpec(memory_space=pl.ANY)] * 7,
        out_specs=[pl.BlockSpec(memory_space=pltpu.VMEM)] * len(outs),
        out_shape=outs,
        scratch_shapes=[
            pltpu.VMEM((panels, rows, width), BF),
            pltpu.VMEM((width, width), F32),
            pltpu.VMEM((poles,), jnp.int32),
            pltpu.VMEM((poles,), F32),
            pltpu.VMEM((roots,), jnp.int32),
            pltpu.VMEM((roots,), F32),
            pltpu.VMEM((roots,), F32),
            pltpu.SemaphoreType.DMA((6,)),
            pltpu.SemaphoreType.DMA((blocks,)),
        ],
        compiler_params=pltpu.CompilerParams(vmem_limit_bytes=16 * MIB),
        cost_estimate=pl.CostEstimate(flops=1, bytes_accessed=1, transcendentals=0),
    )(*[pltpu.with_memory_space_constraint(v, pltpu.HBM) for v in (operands[0], panel_vectors, *operands[1:])])
    return results[:4], results[4:]


def finish_kernel(blocks, start, total, update, project, out_hbm, result, sem):
    block = total.shape[0] // blocks
    row = lax.axis_index("row")
    copies = []
    for code in range(blocks):
        rows = slice(code * block, (code + 1) * block)
        value = total[rows] - jnp.dot(update[rows, start:], project[...], preferred_element_type=F32)
        result[rows] = value.astype(BF)
        at = pl.multiple_of(jnp.bitwise_xor(row, code) * block, block)
        copies.append(pltpu.make_async_copy(result.at[rows], out_hbm.at[pl.ds(at, block)], sem.at[code]))
        copies[-1].start()
    for copy in copies:
        copy.wait()


def finish(blocks, total, update, project, start):
    rows, width = total.shape
    if width % 128:
        result = (total - jnp.dot(update[:, start:], project, preferred_element_type=F32)).astype(BF)
        places = jnp.bitwise_xor(lax.axis_index("row"), jnp.arange(blocks))
        return result.reshape(blocks, -1, width)[places].reshape(rows, width)
    return pl.pallas_call(
        functools.partial(finish_kernel, blocks, start),
        in_specs=[pl.BlockSpec(memory_space=pltpu.VMEM)] * 3,
        out_specs=pl.BlockSpec(memory_space=pl.ANY),
        out_shape=jax.ShapeDtypeStruct((rows, width), BF),
        scratch_shapes=[pltpu.VMEM((rows, width), BF), pltpu.SemaphoreType.DMA((blocks,))],
        compiler_params=pltpu.CompilerParams(vmem_limit_bytes=16 * MIB),
        cost_estimate=pl.CostEstimate(flops=1, bytes_accessed=1, transcendentals=0),
    )(*[pltpu.with_memory_space_constraint(v, pltpu.VMEM) for v in (total, update, project)])


def split_dot(left, right):
    def parts(value):
        if value.dtype == BF:
            return [value]
        high = value.astype(BF)
        return [high, (value - high.astype(F32)).astype(BF)]

    total = None
    for i, a in enumerate(parts(left)):
        for j, b in enumerate(parts(right)):
            if i + j < 2:
                term = jnp.dot(a, b, preferred_element_type=F32)
                total = term if total is None else total + term
    return total


def shards(
    n_row,
    n_col,
    eigvecs,
    pole_order,
    pole_weight,
    root_gap,
    root_shift,
    column_weight,
    panel_vectors,
    panel_factors,
):
    col_orders = bit_orders(n_col, 1)[::-1]
    row_orders = bit_orders(n_row, 0)
    col_stages = len(col_orders[0])
    row_stages = len(row_orders[0])
    rows = eigvecs.shape[0]
    block = rows // n_row
    panel_width = panel_vectors.shape[2]
    parts = n_col // 2
    near = panel_width // parts
    width = root_gap.shape[0] // n_col
    chunks = 2 if width % 256 == 0 else 1
    piece = width // chunks
    sum_order = row_orders[0]
    move_order = sum_order[::-1]

    def swap_cores(value):
        return lax.ppermute(value, "col", [(i, i ^ 1) for i in range(n_col)])

    def swap_col(value, stage):
        return lax.ppermute(value, "col", [(i, i ^ (1 << col_orders[i % 2][stage])) for i in range(n_col)])

    def swap_row(value, bits):
        pairs = [(r * n_col + c, (r ^ (1 << bits[c % 2])) * n_col + c) for r in range(n_row) for c in range(n_col)]
        return lax.ppermute(value, ("row", "col"), pairs)

    def split_targets(value, targets):
        step = targets * block
        kept = [value[i:i + step // 2] for i in range(0, value.shape[0], step)]
        sent = [value[i + step // 2:i + step] for i in range(0, value.shape[0], step)]
        return jnp.concatenate(kept, 0), jnp.concatenate(sent, 0)

    def pick_blocks(value, places):
        return jnp.concatenate([value[i * block:(i + 1) * block] for i in places], 0)

    targets = target_codes(move_order)
    own_codes = list(zip(*[target_codes(order) for order in col_orders]))
    other_codes = [(1 ^ odd, 1 ^ even) for even, odd in own_codes]
    half = len(own_codes) // 2
    operands = (eigvecs, pole_order, pole_weight, root_gap, root_shift, column_weight)
    (vectors, kept, message, correlation), state = panel_blocks(
        targets, row_orders, parts, panel_vectors, operands
    )
    if width % (128 * chunks) or eigvecs.shape[1] % 256:
        state = None
    multiply = functools.partial(
        products, row_codes=targets, parts=n_col, chunks=chunks, operands=operands, state=state
    )
    got_sent, own_sent, made = [], [], ()
    for chunk in range(chunks):
        other, own = multiply([(chunk, other_codes[half:]), (chunk, own_codes[half:])], after=made)
        got_sent.append(swap_cores(other))
        own_sent.append(own)
        made = (own,)
    long = half * piece
    sent = []
    for own, got in zip(own_sent, got_sent):
        (value,) = local(
            lambda own, got: [(own.astype(F32) + got.astype(F32)).astype(BF)],
            [((rows, long), BF)],
            [own, got],
            after=(*made, *sent),
        )
        sent.append(value)
    got = [swap_col(message, 0) for message in sent]
    other_kept = multiply([(chunk, other_codes[:half]) for chunk in range(chunks)], after=(sent[-1],))
    got_kept = [swap_cores(value) for value in other_kept]
    own_kept = multiply([(chunk, own_codes[:half]) for chunk in range(chunks)], after=(other_kept[0],))

    current = [[own, other, new] for own, other, new in zip(own_kept, got_kept, got)]
    for stage in range(1, col_stages):
        long //= 2

        def next_sums(*values, long=long):
            count = len(values) // chunks
            totals = [sum(v.astype(F32) for v in values[i:i + count]) for i in range(0, len(values), count)]
            out = jnp.concatenate([total[:, long:] for total in totals], 1).astype(BF)
            return *[total[:, :long] for total in totals], out

        *totals, col_message = local(
            next_sums,
            [((rows, long), F32)] * chunks + [((rows, chunks * long), BF)],
            sum(current, []),
        )
        if stage == 1:
            first_message = col_message
        got = swap_col(col_message, stage)
        current = [[total, got] for total in totals]
        if stage < col_stages - 1:
            current = [[total, got[:, i * long:(i + 1) * long]] for i, total in enumerate(totals)]

    for stage in range(row_stages):
        panel_got = swap_row(message, [order[stage] for order in row_orders])

        if stage < row_stages - 1:

            def next_panel(kept, correlation, got, targets=n_row >> (stage + 1)):
                correlation = correlation + got[:near].astype(F32)
                kept, moved = split_targets(jnp.concatenate([kept, got[near:]], 0), targets)
                return kept, jnp.concatenate([correlation.astype(BF), moved], 0), correlation

            kept, message, correlation = local(
                next_panel,
                [((rows // 2, panel_width), BF), ((near + rows // 2, panel_width), BF), ((near, panel_width), F32)],
                [kept, correlation, panel_got],
                after=(sent[-1],),
                cost=5000000000,
            )
    panel_places = [[source_codes(order).index(code) for code in range(n_row)] for order in row_orders]

    first_rows = 3 * rows // 4

    def panel_done(kept, correlation, got):
        correlation = (correlation + got[:near].astype(F32)).astype(BF)
        value = jnp.concatenate([kept, got[near:]], 0)
        orders = [pick_blocks(value, places).astype(F32) for places in panel_places]
        value = jnp.where(is_even(), orders[0], orders[1]).astype(BF)
        return value, correlation, value[:first_rows], value[first_rows:]

    mine, correlation, *mine_sent = local(
        panel_done,
        [((r, panel_width), BF) for r in (rows, near, first_rows, rows - first_rows)],
        [kept, correlation, panel_got],
        after=(first_message,),
    )
    other = [swap_cores(value) for value in mine_sent]

    wide = 2 * panel_width
    summed = wide // 2 if row_stages > 1 else wide

    def projections(mine, *values):
        other, values = values[:2], values[2:]
        merged = jnp.concatenate(values[:chunks], 1) + jnp.concatenate(values[chunks:], 1).astype(F32)
        merged = merged.astype(BF)
        dims = (((0,), (0,)), ((), ()))
        project = jnp.concatenate(
            [
                lax.dot_general(pick_blocks(v, targets), merged, dims, preferred_element_type=F32)
                for v in (mine, jnp.concatenate(other, 0))
            ],
            0,
        )
        project = swap_groups(project, 0, sum_order)
        out = project if row_stages == 1 else project[summed:]
        return project[:summed], out.astype(BF), *split_targets(merged, n_row)

    shapes = lambda size: [((size, width), F32), ((size, width), BF)]
    halves = [((rows // 2, width), BF)] * 2
    last_got = [current[0][1]] if col_stages > 1 else [c[1] for c in current]
    project, message, blocks, moved = local(
        projections,
        shapes(summed) + halves,
        [mine, *other, *[c[0] for c in current], *last_got],
    )
    project_got = swap_row(message, [sum_order[0]] * 2)
    blocks_got = swap_row(moved, [move_order[0]] * 2)

    def join(mine, got, stage):
        shift = select_code(is_even(), (col_orders[0][stage], col_orders[1][stage]))
        low = jnp.bitwise_and(lax.shift_right_logical(lax.axis_index("col"), shift), 1) == 0
        mine, got = mine.astype(F32), got.astype(F32)
        return jnp.concatenate([jnp.where(low, mine, got), jnp.where(low, got, mine)], 0)

    joined = near
    for stage in range(col_stages - 1):
        joined *= 2
        (correlation,) = local(
            lambda mine, got, stage=stage: [join(mine, got, stage).astype(BF)],
            [((joined, panel_width), BF)],
            [correlation, swap_col(correlation, stage)],
            after=(message,),
        )
    other_correlation = swap_col(correlation, col_stages - 1)
    part_orders = [source_codes([bit - 1 for bit in order]) for order in col_orders]
    part_orders = [[order.index(part) for part in range(parts)] for order in part_orders]

    def update_factor(vectors, factors, mine, other):
        even = is_even()
        correlation = join(mine, other, col_stages - 1)
        ordered = [
            jnp.concatenate([correlation[i * near:(i + 1) * near] for i in order], 0) for order in part_orders
        ]
        correlation = jnp.where(even, ordered[0], ordered[1]).astype(BF)
        across = split_dot(vectors[1], split_dot(factors[1], correlation))
        first = split_dot(vectors[0].astype(F32) - across, factors[0])
        second = split_dot(vectors[1], factors[1])
        update = jnp.concatenate([jnp.where(even, first, second), jnp.where(even, second, first)], 1)
        return [swap_groups(update, 1, sum_order).astype(BF)]

    for stage in range(1, row_stages):
        last = stage == row_stages - 1
        size = summed if last else summed // 2

        def next_project(project, got, last=last, size=size):
            total = project + got.astype(F32)
            return total[:size], (total if last else total[size:]).astype(BF)

        project, message = local(
            next_project, shapes(size), [project, project_got], after=(correlation,) if stage == 1 else ()
        )
        project_got = swap_row(message, [sum_order[stage]] * 2)
        summed = size
    (update,) = local(
        update_factor,
        [((rows, wide), BF)],
        [vectors, panel_factors, correlation, other_correlation],
        after=(message,),
        cost=1000000000,
    )

    for stage in range(1, row_stages):
        blocks, moved = local(
            lambda blocks, got, targets=n_row >> stage: split_targets(jnp.concatenate([blocks, got], 0), targets),
            halves,
            [blocks, blocks_got],
        )
        blocks_got = swap_row(moved, [move_order[stage]] * 2)
    move_places = [source_codes(move_order).index(code) for code in range(n_row)]
    (cyclic,) = local(
        lambda blocks, got: [pick_blocks(jnp.concatenate([blocks, got], 0), move_places)],
        [((rows, width), BF)],
        [blocks, blocks_got],
    )
    (project,) = local(
        lambda project, got: [(project + got.astype(F32)).astype(BF)],
        [((summed, width), BF)],
        [project, project_got],
    )
    (total,) = local(
        lambda update, cyclic, project: [
            cyclic.astype(F32) - jnp.dot(update[:, :summed], project, preferred_element_type=F32)
        ],
        [((rows, width), F32)],
        [update, cyclic, project],
        cost=1000000000,
    )
    for stage in reversed(range(row_stages - 1)):
        got = swap_row(project, [sum_order[stage]] * 2)
        project = got if row_stages == 2 else jnp.concatenate([project, got], 0)
    rest = project if row_stages == 2 else project[summed:]
    return finish(n_row, total, update, rest, summed)


def solution(mesh):
    return jax.shard_map(
        functools.partial(shards, mesh.shape["row"], mesh.shape["col"]),
        mesh=mesh,
        in_specs=(P("row", "col"), P("col"), P("col"), P(), P(), P(), P(None, "row", None), P()),
        out_specs=P("row", "col"),
        check_vma=False,
    )
```
